128 devices in a mesh: dp: 16 (over y_lo, x, core), slab: 8 (over y_hi, z).
Axes of the slice: x: 4, y: 4 (y_hi: 2, y_lo: 2; y = y_hi * 2 + y_lo), z: 4, core: 2. Of those that a mesh axis runs over, the one named last changes fastest.
Arguments:
- latents: bfloat16 [16, 128, 512, 128], P('dp', 'slab'), may hold values from -6 to 6
- image_grad: bfloat16 [16, 3, 128, 512], P('dp', None, 'slab'), may hold values from -6 to 6
- heights: int32 [16], P('dp'), may hold values from 64 to 128, as said below
- widths: int32 [16], P('dp'), may hold values from 256 to 512, as said below
- buckets: int32 [16], P('dp'), may hold values from 0 to 7
- bucket_scale: float32 [8], replicated, may hold values from 0.5 to 2
- conv_first: bfloat16 [1152, 128], replicated, may hold values from -0.1875 to 0.1875
- conv_second: bfloat16 [1152, 128], replicated, may hold values from -0.1875 to 0.1875
- conv_image: bfloat16 [3, 1152], replicated, may hold values from -0.1875 to 0.1875
- norm_gain: float32 [128], replicated, may hold values from 0.5 to 1.5
- norm_bias: float32 [128], replicated, may hold values from -3 to 3
Outputs:
- grad_conv_first: float32 [1152, 128], P('dp')
- grad_conv_second: float32 [1152, 128], P('dp')
- grad_conv_image: float32 [3, 1152], replicated
- grad_norm_gain: float32 [128], replicated
- grad_norm_bias: float32 [128], replicated
- grad_latents: bfloat16 [16, 128, 512, 128], P('dp', 'slab')
The draws below stay inside these ranges and needn't reach their ends.
Inputs may be any that keep to these rules, and one draw needn't show every extreme that they name: `heights`: some image has exactly 128 rows. `widths`: some image has exactly 512 columns.
All inputs are finite; a program needn't handle non-finite values.
Results may differ from the reference program's by a relative error of at most 0.0078.
Values may be sent and summed in bfloat16 or wider, within the bound.
A program may use at most 192 MiB of HBM per device.

```python
import math
import jax
import jax.numpy as jnp
from jax import lax

CHANNELS = 128
GROUPS = 32
WIDTH = 512
NBUCKET = 8
IMAGES = 16
HEIGHT = 128


def draw_heights(key, part):
    key = jax.random.fold_in(key, 11)
    first, second = jax.random.split(key)
    values = jax.random.randint(first, (IMAGES,), HEIGHT // 2, HEIGHT + 1)
    tallest = jax.random.randint(second, (), 0, IMAGES)
    return jnp.where(jnp.arange(IMAGES) == tallest, HEIGHT, values).astype(jnp.int32)


def draw_widths(key, part):
    key = jax.random.fold_in(key, 23)
    first, second = jax.random.split(key)
    values = jax.random.randint(first, (IMAGES,), WIDTH // 2, WIDTH + 1)
    widest = jax.random.randint(second, (), 0, IMAGES)
    return jnp.where(jnp.arange(IMAGES) == widest, WIDTH, values).astype(jnp.int32)


def set_ends(result, own_key, least, largest):
    dims = result.shape
    place = [jax.random.randint(jax.random.fold_in(own_key, axis), (), 0, dims[axis]) for axis in range(len(dims))]
    result = result.at[tuple(place)].set(least)
    longest = dims.index(max(dims))
    place[longest] = (place[longest] + 1) % dims[longest]
    return result.at[tuple(place)].set(largest)


def steps_of(key, dims, shards, low, high):
    loudness, own = 1.0, jax.random.fold_in(key, 6)
    for dim, parts in shards:
        steps = jnp.exp(jax.random.uniform(jax.random.fold_in(own, dim), (parts,), jnp.float32, low / len(shards), high / len(shards)))
        loudness = loudness * jnp.repeat(steps, dims[dim] // parts).reshape([-1 if axis == dim else 1 for axis in range(len(dims))])
    return loudness


def gaussian(rng, extent, scale, bound, cuts=(), kind=jnp.bfloat16):
    drawn = scale * jax.random.normal(rng, extent, jnp.float32)
    if cuts:
        drawn = drawn * steps_of(rng, extent, cuts, -0.22, 0.18)
    return jnp.clip(drawn, -bound, bound).astype(kind)


def setup_inputs(seed: int = 0) -> dict:
    key_of = jax.random.split(jax.random.key(seed), 12)
    return {
        "latents": gaussian(key_of[0], (IMAGES, HEIGHT, WIDTH, CHANNELS), 1.0, 6.0, ((0, 16), (1, 8))),
        "image_grad": gaussian(key_of[1], (IMAGES, 3, HEIGHT, WIDTH), 1.0, 6.0, ((0, 16), (2, 8))),
        "heights": draw_heights(jax.random.fold_in(key_of[11], 71), 0),
        "widths": draw_widths(jax.random.fold_in(key_of[11], 71), 0),
        "buckets": set_ends(jax.random.randint(key_of[4], (IMAGES,), 0, NBUCKET), jax.random.fold_in(key_of[4], 1), 0, NBUCKET - 1).astype(jnp.int32),
        "bucket_scale": jnp.clip(jnp.exp(jax.random.uniform(key_of[5], (NBUCKET,), jnp.float32, math.log(0.5), math.log(2.0))), 0.5, 2.0),
        "conv_first": gaussian(key_of[6], (9 * CHANNELS, CHANNELS), (9 * CHANNELS) ** -0.5, 0.1875),
        "conv_second": gaussian(key_of[7], (9 * CHANNELS, CHANNELS), (9 * CHANNELS) ** -0.5, 0.1875),
        "conv_image": gaussian(key_of[8], (3, 9 * CHANNELS), (9 * CHANNELS) ** -0.5, 0.1875),
        "norm_gain": jnp.clip(1.0 + 0.1 * jax.random.normal(key_of[9], (CHANNELS,), jnp.float32), 0.5, 1.5),
        "norm_bias": gaussian(key_of[10], (CHANNELS,), 0.5, 3.0, (), jnp.float32),
    }


norm_eps = 1e-06

def silu_slope(value):
    sigma = jax.nn.sigmoid(value)
    return sigma * (1.0 + value * (1.0 - sigma))

def conv_rows(extended, weight):
    chan_in = extended.shape[-1]
    out_rows = extended.shape[-3] - 2
    col_count = extended.shape[-2]
    padded = jnp.pad(extended, [(0, 0)] * (extended.ndim - 2) + [(1, 1), (0, 0)])
    total = jnp.zeros(extended.shape[:-3] + (out_rows, col_count, weight.shape[1]), jnp.float32)
    for tap_index in range(9):
        row_off, col_off = divmod(tap_index, 3)
        piece = padded[..., row_off:row_off + out_rows, col_off:col_off + col_count, :]
        block = weight[tap_index * chan_in:(tap_index + 1) * chan_in]
        total = total + jnp.dot(piece, block, preferred_element_type=jnp.float32)
    return total

def data_grad(extended, weight):
    chan_in = weight.shape[0] // 9
    out_rows = extended.shape[-3] - 2
    col_count = extended.shape[-2]
    padded = jnp.pad(extended, [(0, 0)] * (extended.ndim - 2) + [(1, 1), (0, 0)])
    total = jnp.zeros(extended.shape[:-3] + (out_rows, col_count, chan_in), jnp.float32)
    for tap_index in range(9):
        row_off, col_off = divmod(tap_index, 3)
        piece = padded[..., 2 - row_off:2 - row_off + out_rows, 2 - col_off:2 - col_off + col_count, :]
        block = weight[tap_index * chan_in:(tap_index + 1) * chan_in]
        total = total + jnp.dot(piece, block.T, preferred_element_type=jnp.float32)
    return total

def weight_grad(extended, cotangent):
    out_rows = extended.shape[-3] - 2
    col_count = extended.shape[-2]
    padded = jnp.pad(extended, [(0, 0)] * (extended.ndim - 2) + [(1, 1), (0, 0)])
    leading = tuple(range(cotangent.ndim - 1))
    pieces = []
    for tap_index in range(9):
        row_off, col_off = divmod(tap_index, 3)
        piece = padded[..., row_off:row_off + out_rows, col_off:col_off + col_count, :]
        pieces.append(lax.dot_general(piece, cotangent, ((leading, leading), ((), ())), preferred_element_type=jnp.float32))
    return jnp.concatenate(pieces, axis=0)

def group_sum(values):
    return lax.optimization_barrier(jnp.sum(values, axis=(0, 1))).reshape(GROUPS, -1).sum(-1)

def reference(latents, image_grad, heights, widths, buckets, bucket_scale, conv_first, conv_second, conv_image, norm_gain, norm_bias):
    pixel_scale = 1.0 / math.sqrt(IMAGES * HEIGHT * WIDTH)
    picked = lax.optimization_barrier(jnp.sum(jnp.where(buckets[:, None] == jnp.arange(NBUCKET)[None, :], bucket_scale[None, :], 0.0), axis=1))
    per_group = CHANNELS // GROUPS

    def pad_rows(value, axis):
        spec = [(0, 0)] * value.ndim
        spec[axis] = (1, 1)
        return jnp.pad(value, spec)

    def one_image(carry, inputs):
        latent, grad_image, height, col_limit, weight_scale = inputs
        row_index = jnp.arange(HEIGHT)
        col_index = jnp.arange(WIDTH)
        valid = ((row_index[:, None] < height) & (col_index[None, :] < col_limit)).astype(jnp.float32)
        inside = valid[:, :, None]
        latent_f = latent.astype(jnp.float32)
        input_act = (jax.nn.silu(latent_f) * inside).astype(jnp.bfloat16)
        hidden_one = conv_rows(pad_rows(input_act, 0), conv_first).astype(jnp.bfloat16)
        hidden_one_f = hidden_one.astype(jnp.float32)
        middle_act = (jax.nn.silu(hidden_one_f) * inside).astype(jnp.bfloat16)
        hidden_two = latent_f + conv_rows(pad_rows(middle_act, 0), conv_second)
        count = (height * col_limit * per_group).astype(jnp.float32)
        masked = hidden_two * inside
        group_mean = group_sum(masked) / count
        group_rstd = lax.rsqrt(group_sum(masked * hidden_two) / count - group_mean * group_mean + norm_eps)
        mean_wide = jnp.repeat(group_mean, per_group)
        rstd_wide = jnp.repeat(group_rstd, per_group)
        normed = (hidden_two - mean_wide) * rstd_wide
        shaped = normed * norm_gain + norm_bias
        norm_act = (jax.nn.silu(shaped) * inside).astype(jnp.bfloat16)
        grad_img = (grad_image.astype(jnp.float32) * weight_scale * valid[None]).astype(jnp.bfloat16)
        norm_pad = jnp.pad(pad_rows(norm_act, 0), ((0, 0), (1, 1), (0, 0)))
        grad_pad = jnp.pad(pad_rows(grad_img, 1), ((0, 0), (0, 0), (1, 1)))
        image_terms = []
        grad_norm_act = jnp.zeros((HEIGHT, WIDTH, CHANNELS), jnp.float32)
        for tap_index in range(9):
            row_off, col_off = divmod(tap_index, 3)
            piece = norm_pad[row_off:row_off + HEIGHT, col_off:col_off + WIDTH, :]
            image_terms.append(lax.dot_general(grad_img, piece, (((1, 2), (0, 1)), ((), ())), preferred_element_type=jnp.float32))
            back_piece = grad_pad[:, 2 - row_off:2 - row_off + HEIGHT, 2 - col_off:2 - col_off + WIDTH]
            block = conv_image[:, tap_index * CHANNELS:(tap_index + 1) * CHANNELS]
            grad_norm_act = grad_norm_act + lax.dot_general(back_piece, block, (((0,), (0,)), ((), ())), preferred_element_type=jnp.float32)
        grad_conv_image = jnp.concatenate(image_terms, axis=1)
        grad_shaped = grad_norm_act * inside * silu_slope(shaped)
        gain_term = lax.optimization_barrier(jnp.sum(grad_shaped * normed, axis=(0, 1)))
        bias_term = lax.optimization_barrier(jnp.sum(grad_shaped, axis=(0, 1)))
        grad_normed = grad_shaped * norm_gain
        first_back = group_sum(grad_normed) / count
        second_back = group_sum(grad_normed * normed) / count
        grad_two = (rstd_wide * (grad_normed - jnp.repeat(first_back, per_group) - normed * jnp.repeat(second_back, per_group)) * inside).astype(jnp.bfloat16)
        grad_conv_second = weight_grad(pad_rows(middle_act, 0), grad_two)
        grad_middle = data_grad(pad_rows(grad_two, 0), conv_second)
        grad_one = (grad_middle * inside * silu_slope(hidden_one_f)).astype(jnp.bfloat16)
        grad_conv_first = weight_grad(pad_rows(input_act, 0), grad_one)
        grad_input = data_grad(pad_rows(grad_one, 0), conv_first)
        grad_latent = (grad_two.astype(jnp.float32) + grad_input * inside * silu_slope(latent_f)).astype(jnp.bfloat16)
        carry = (carry[0] + grad_conv_first, carry[1] + grad_conv_second, carry[2] + grad_conv_image, carry[3] + gain_term, carry[4] + bias_term)
        return (carry, grad_latent)
    init = (jnp.zeros((9 * CHANNELS, CHANNELS), jnp.float32), jnp.zeros((9 * CHANNELS, CHANNELS), jnp.float32), jnp.zeros((3, 9 * CHANNELS), jnp.float32), jnp.zeros((CHANNELS,), jnp.float32), jnp.zeros((CHANNELS,), jnp.float32))
    totals, grad_latents = lax.scan(one_image, init, (latents, image_grad, heights, widths, picked))
    return (totals[0] * pixel_scale, totals[1] * pixel_scale, totals[2] * pixel_scale, totals[3] * pixel_scale, totals[4] * pixel_scale, grad_latents)
```

```python
import functools
import math

import jax
import jax.numpy as jnp
from jax import lax
from jax.experimental import pallas as pl
from jax.experimental.pallas import tpu as pltpu
from jax.sharding import PartitionSpec as P

MESH = pl.DeviceIdType.MESH
F32 = jnp.float32
BF16 = jnp.bfloat16
PER_GROUP = 4
NORM_EPS = 1e-06
S = 16
C = 128


def dot(a, b):
    return jnp.dot(a, b, preferred_element_type=F32)


def sigmoid(v):
    return 0.5 * jnp.tanh(0.5 * v) + 0.5


def group_total(v):
    lane = lax.broadcasted_iota(jnp.int32, v.shape, 1)
    v = v + jnp.where(lane % 2 == 0, pltpu.roll(v, C - 1, 1), pltpu.roll(v, 1, 1))
    return v + jnp.where(lane % 4 < 2, pltpu.roll(v, C - 2, 1), pltpu.roll(v, 2, 1))


def kernel(
    ndp, nslab, rows, width, pixel_scale,
    lat_ref, img_ref, h_ref, w_ref, bk_ref, bs_ref, w1_ref, w2_ref, ci_ref, gain_ref, bias_ref,
    gw1_ref, gw2_ref, gci_ref, gg_ref, gb_ref, gl_ref,
    perm, permt, col, latp, act, mid, actt, midt, h1, h2, gs, nact, b2, b1,
    w4, ci4f, ci4, gstage, gimg, acc, flat, imgacc, sums, stat_send, stat_recv,
    send_a, recv_a, send_b, recv_b, small_a, small_ra, small_b, small_rb,
    halo_s, halo_r, stat_ss, stat_rs, a_ss, a_rs, b_ss, b_rs,
):
    t_count = width // S
    last = rows + 1
    npair = rows // 2
    blk = (9 * C) // ndp
    dp = lax.axis_index("dp")
    slab = lax.axis_index("slab")

    barrier = pltpu.get_barrier_semaphore()

    def greet(axis, me, n):
        def body(off, _):
            pl.semaphore_signal(
                barrier, inc=1, device_id={axis: lax.rem(me + off, n)}, device_id_type=MESH
            )
            return 0
        lax.fori_loop(1, n, body, 0)

    greet("slab", slab, nslab)
    greet("dp", dp, ndp)

    height = h_ref[0]
    limit = w_ref[0]
    count = (height * limit * PER_GROUP).astype(F32)

    def inside(r):
        return col[...] < jnp.where(slab * rows + r < height, limit, 0)

    def loop(lo, hi, body):
        def step(i, _):
            body(i)
            return 0
        lax.fori_loop(lo, hi, step, 0)

    def put(ref, row, a):
        ref[row, 1:t_count + 1] = a.reshape(t_count, S, C)
        sub = lax.broadcasted_iota(jnp.int32, (S, C), 0)
        low = pltpu.roll(a[width - S:].astype(F32), 1, 0)
        ref[row, 0] = jnp.where(sub == 0, 0.0, low).astype(BF16)
        high = pltpu.roll(a[:S].astype(F32), S - 1, 0)
        ref[row, t_count + 1] = jnp.where(sub == S - 1, 0.0, high).astype(BF16)

    def halo(ref, e, d):
        if d == 0:
            src, dst, to = 1, last, lax.rem(slab + nslab - 1, nslab)
        else:
            src, dst, to = last - 1, 0, lax.rem(slab + 1, nslab)
        return pltpu.make_async_remote_copy(
            src_ref=ref.at[src], dst_ref=ref.at[dst],
            send_sem=halo_s.at[e, d], recv_sem=halo_r.at[e, d],
            device_id={"slab": to}, device_id_type=MESH,
        )

    def halo_start(ref, e):
        for d in range(2):
            halo(ref, e, d).start()

    def halo_wait(ref, e):
        for d in range(2):
            halo(ref, e, d).wait()

        @pl.when(slab == 0)
        def _():
            ref[0] = jnp.zeros(ref.shape[1:], ref.dtype)

        @pl.when(slab == nslab - 1)
        def _():
            ref[last] = jnp.zeros(ref.shape[1:], ref.dtype)

    def spread(src_of, recv, ss, rs, e, axis, me, n):
        def copy(peer, slot):
            return pltpu.make_async_remote_copy(
                src_ref=src_of(peer), dst_ref=recv.at[slot],
                send_sem=ss.at[e, peer], recv_sem=rs.at[e, slot],
                device_id={axis: peer}, device_id_type=MESH,
            )

        def start():
            def body(off):
                copy(lax.rem(me + off, n), me).start()
            loop(1, n, body)

        def wait():
            def body(off):
                peer = lax.rem(me + off, n)
                copy(peer, peer).wait_recv()
                copy(peer, me).wait_send()
            loop(1, n, body)

        return start, wait

    a_i = lax.broadcasted_iota(jnp.int32, (width, width), 0)
    b_i = lax.broadcasted_iota(jnp.int32, (width, width), 1)
    perm[...] = jnp.where((a_i % S) * t_count + a_i // S == b_i, 1.0, 0.0).astype(BF16)
    permt[...] = jnp.where((b_i % S) * t_count + b_i // S == a_i, 1.0, 0.0).astype(BF16)
    j_i = lax.broadcasted_iota(jnp.int32, (width, C), 0)
    col[...] = (j_i % S) * t_count + j_i // S

    def stage_input(i):
        x = dot(perm[...], jnp.concatenate([lat_ref[2 * i], lat_ref[2 * i + 1]], axis=1))
        for k in range(2):
            r = 2 * i + k
            v = x[:, k * C:(k + 1) * C]
            latp[r] = v.astype(BF16)
            a = jnp.where(inside(r), v * sigmoid(v), 0.0).astype(BF16)
            put(act, r + 1, a)
            actt[r + 1] = a.T

    loop(0, npair, stage_input)

    scale = bs_ref[bk_ref[0]]
    row3 = lax.broadcasted_iota(jnp.int32, (3, rows, width), 1) + slab * rows
    lane3 = lax.broadcasted_iota(jnp.int32, (3, rows, width), 2)
    graded = jnp.where((row3 < height) & (lane3 < limit), img_ref[...].astype(F32) * scale, 0.0)
    graded = graded.reshape(3 * rows, width)
    lane = lax.broadcasted_iota(jnp.int32, (3 * rows, width), 1)
    shifted = [
        jnp.where(lane == width - 1, 0.0, pltpu.roll(graded, width - 1, 1)),
        graded,
        jnp.where(lane == 0, 0.0, pltpu.roll(graded, 1, 1)),
    ]
    stacked = jnp.concatenate([s.astype(BF16) for s in shifted], axis=0)
    gstage[...] = jnp.zeros_like(gstage)
    placed = dot(stacked, permt[...])
    for k in range(width // C):
        gstage[k, 0:9 * rows] = placed[:, k * C:(k + 1) * C]
        for r in range(rows):
            gimg[r + 1, :, k * C:(k + 1) * C] = gstage[k, pl.ds(r, 16, stride=rows), :].astype(BF16)

    pl.semaphore_wait(barrier, ndp + nslab - 2)
    halo_start(act, 0)
    halo_start(gimg, 1)

    for c, (ref, flip) in enumerate(((w1_ref, False), (w2_ref, False), (w2_ref, True), (w1_ref, True))):
        for j in range(4):
            for q in range(3):
                at = (j * 3 + q) * C
                for k in range(2):
                    if 0 <= j - k <= 2:
                        tap = 3 * (j - k) + q
                        if flip:
                            b = ref[(8 - tap) * C:(9 - tap) * C, :].T
                        else:
                            b = ref[tap * C:(tap + 1) * C, :]
                    else:
                        b = jnp.zeros((C, C), BF16)
                    w4[c, at:at + C, k * C:(k + 1) * C] = b
    ci4f[...] = jnp.zeros_like(ci4f)
    for p in range(3):
        for q in range(3):
            piece = ci_ref[:, (3 * p + q) * C:(3 * p + q + 1) * C].astype(F32)
            for k in range(2):
                at = (2 - p + k) * 16 + q * 3
                ci4f[at:at + 3, k * C:(k + 1) * C] = piece
    ci4[...] = ci4f[...].astype(BF16)

    def conv(src, c, i):
        taps = [
            src[2 * i + j, q:q + t_count].reshape(width, C) for j in range(4) for q in range(3)
        ]
        return dot(jnp.concatenate(taps, axis=1), w4[c])

    def ends(body):
        loop(0, 2, lambda k: body(k * (npair - 1)))

    def stage_one(i):
        y = conv(act, 0, i)
        for k in range(2):
            r = 2 * i + k
            hb = y[:, k * C:(k + 1) * C].astype(BF16)
            h1[r] = hb
            hf = hb.astype(F32)
            m = jnp.where(inside(r), hf * sigmoid(hf), 0.0).astype(BF16)
            put(mid, r + 1, m)
            midt[r + 1] = m.T

    loop(1, npair - 1, stage_one)
    halo_wait(act, 0)
    ends(stage_one)
    halo_start(mid, 2)
    for e in (0, last):
        actt[e] = act[e, 1:t_count + 1].reshape(width, C).T

    sums[...] = jnp.zeros_like(sums)

    def fold(v):
        return jnp.sum(v.reshape(width // 8, 8, C), axis=0)

    def stage_two(i):
        y = conv(mid, 1, i)
        for k in range(2):
            r = 2 * i + k
            v = y[:, k * C:(k + 1) * C] + latp[r].astype(F32)
            h2[r] = v
            masked = jnp.where(inside(r), v, 0.0)
            sums[0] += fold(masked)
            sums[1] += fold(masked * v)

    loop(1, npair - 1, stage_two)
    halo_wait(mid, 2)
    ends(stage_two)

    def stats(e):
        stat_send[e, 0:1] = jnp.sum(sums[2 * e], axis=0, keepdims=True)
        stat_send[e, 1:2] = jnp.sum(sums[2 * e + 1], axis=0, keepdims=True)
        stat_recv[e, slab] = stat_send[e]
        return spread(
            lambda peer: stat_send.at[e], stat_recv.at[e], stat_ss, stat_rs, e, "slab", slab, nslab
        )

    def stat_total(e):
        total = stat_recv[e, 0]
        for k in range(1, nslab):
            total = total + stat_recv[e, k]
        return total

    for e in range(2):
        stat_send[e] = jnp.zeros(stat_send.shape[1:], F32)
    start, wait = stats(0)
    start()

    halo_wait(gimg, 1)

    def stage_image(i):
        y = lax.dot_general(
            gimg[pl.ds(2 * i, 4)].reshape(64, width), ci4[...], (((0,), (0,)), ((), ())),
            preferred_element_type=F32,
        )
        for k in range(2):
            gs[2 * i + k] = y[:, k * C:(k + 1) * C]

    loop(0, npair, stage_image)
    for e in (0, last):
        midt[e] = mid[e, 1:t_count + 1].reshape(width, C).T
    wait()

    total = stat_total(0)
    mean = group_total(total[0:1]) / count
    rstd = lax.rsqrt(group_total(total[1:2]) / count - mean * mean + NORM_EPS)
    gain = gain_ref[...]
    bias = bias_ref[...]

    def stage_norm(r):
        n = (h2[r] - mean) * rstd
        v = n * gain + bias
        s = sigmoid(v)
        vs = v * s
        here = inside(r)
        nact[r] = jnp.where(here, vs, 0.0).astype(BF16)
        g = jnp.where(here, gs[r] * (s + vs * (1.0 - s)), 0.0)
        h2[r] = n
        gs[r] = g
        sums[2] += fold(g)
        sums[3] += fold(g * n)

    loop(0, rows, stage_norm)
    start, wait = stats(1)
    start()

    imgacc[...] = jnp.zeros_like(imgacc)

    def stage_imgw(i):
        imgacc[...] += dot(
            gimg[pl.ds(2 * i, 4)].reshape(64, width),
            jnp.concatenate([nact[2 * i], nact[2 * i + 1]], axis=1),
        )

    loop(0, npair, stage_imgw)
    small_a[...] = imgacc[0:48, 0:C] + imgacc[16:64, C:2 * C]
    small_a[9:11] = jnp.concatenate(
        [jnp.sum(sums[3], axis=0, keepdims=True), jnp.sum(sums[2], axis=0, keepdims=True)], axis=0
    )
    small_ra[dp] = small_a[...]
    small_start, small_wait = spread(
        lambda peer: small_a, small_ra, a_ss, a_rs, 0, "dp", dp, ndp
    )
    wait()
    small_start()

    total = stat_total(1)
    c1 = rstd * gain
    c0 = rstd * (group_total(total[0:1] * gain) / count)
    c2 = rstd * (group_total(total[1:2] * gain) / count)

    def stage_grad_two(r):
        g = jnp.where(inside(r), gs[r] * c1 - c0 - h2[r] * c2, 0.0).astype(BF16)
        put(b2, r + 1, g)

    loop(0, 2, lambda k: stage_grad_two(k * (rows - 1)))
    halo_start(b2, 3)
    loop(1, rows - 1, stage_grad_two)

    def weight_grad(at, b):
        acc[...] = jnp.zeros_like(acc)

        def piece(row, q):
            return b[row, 2 - q:2 - q + t_count].reshape(width, C)

        def body(i):
            lhs = jnp.concatenate(
                [at[pl.ds(2 * i + k, 3)].reshape(3 * C, width) for k in range(2)], axis=1
            )
            rhs = jnp.concatenate(
                [
                    jnp.concatenate([piece(2 * i + 1 + k, q) for q in range(2)], axis=1)
                    for k in range(2)
                ],
                axis=0,
            )
            acc[:, 0:2 * C] += dot(lhs, rhs)
            rhs = jnp.concatenate([piece(2 * i + 1 + k, 2) for k in range(2)], axis=1)
            z = dot(at[pl.ds(2 * i, 4)].reshape(4 * C, width), rhs)
            acc[:, 2 * C:] += z[0:3 * C, 0:C] + z[C:, C:]

        loop(0, npair, body)

    def scatter(e):
        for p in range(3):
            for q in range(3):
                flat[(3 * p + q) * C:(3 * p + q + 1) * C] = acc[p * C:(p + 1) * C, q * C:(q + 1) * C]

        def body(d):
            send_a[e, d, 0:blk] = flat[pl.ds(pl.multiple_of(d * blk, 8), blk)].astype(BF16)
        loop(0, ndp, body)
        recv_a[e, dp] = send_a[e, dp]
        return spread(
            lambda peer: send_a.at[e, peer], recv_a.at[e], a_ss, a_rs, 1 + e, "dp", dp, ndp
        )

    def gather(e):
        part = recv_a[e, 0].astype(F32)
        for k in range(1, ndp):
            part = part + recv_a[e, k].astype(F32)
        send_b[e] = part.astype(BF16)
        recv_b[e, slab] = send_b[e]
        return spread(lambda peer: send_b.at[e], recv_b.at[e], b_ss, b_rs, 1 + e, "slab", slab, nslab)

    def finish(e, out):
        part = recv_b[e, 0].astype(F32)
        for k in range(1, nslab):
            part = part + recv_b[e, k].astype(F32)
        out[...] = part[0:blk] * pixel_scale

    send_a[...] = jnp.zeros_like(send_a)
    weight_grad(midt, b2)
    second_start, second_wait = scatter(0)
    second_start()

    halo_wait(b2, 3)

    def stage_grad_one(i):
        y = conv(b2, 2, i)
        for k in range(2):
            r = 2 * i + k
            v = h1[r].astype(F32)
            s = sigmoid(v)
            slope = s + v * s * (1.0 - s)
            g = jnp.where(inside(r), y[:, k * C:(k + 1) * C] * slope, 0.0).astype(BF16)
            put(b1, r + 1, g)

    ends(stage_grad_one)
    halo_start(b1, 4)
    loop(1, npair - 1, stage_grad_one)

    small_wait()
    part = small_ra[0]
    for k in range(1, ndp):
        part = part + small_ra[k]
    small_b[...] = part
    small_rb[slab] = part
    small_b_start, small_b_wait = spread(
        lambda peer: small_b, small_rb, b_ss, b_rs, 0, "slab", slab, nslab
    )
    small_b_start()
    second_wait()
    second_b_start, second_b_wait = gather(0)
    second_b_start()

    weight_grad(actt, b1)
    first_start, first_wait = scatter(1)
    first_start()
    halo_wait(b1, 4)

    def stage_latents(i):
        y = conv(b1, 3, i)
        done = []
        for k in range(2):
            r = 2 * i + k
            v = latp[r].astype(F32)
            s = sigmoid(v)
            slope = s + v * s * (1.0 - s)
            g = jnp.where(inside(r), y[:, k * C:(k + 1) * C] * slope, 0.0)
            own = b2[r + 1, 1:t_count + 1].reshape(width, C).astype(F32)
            done.append((own + g).astype(BF16))
        z = dot(permt[...], jnp.concatenate(done, axis=1)).astype(BF16)
        for k in range(2):
            gl_ref[2 * i + k] = z[:, k * C:(k + 1) * C]

    half = npair * 3 // 4
    loop(0, half, stage_latents)
    first_wait()
    first_b_start, first_b_wait = gather(1)
    first_b_start()
    loop(half, npair, stage_latents)

    small_b_wait()
    part = small_rb[0]
    for k in range(1, nslab):
        part = part + small_rb[k]
    part = part * pixel_scale
    gg_ref[...] = part[9:10]
    gb_ref[...] = part[10:11]
    for p in range(3):
        for q in range(3):
            at = (2 - p) * 16 + q * 3
            gci_ref[:, (3 * p + q) * C:(3 * p + q + 1) * C] = part[at:at + 3]
    second_b_wait()
    finish(0, gw2_ref)
    first_b_wait()
    finish(1, gw1_ref)


def shards(
    latents, image_grad, heights, widths, buckets, bucket_scale,
    conv_first, conv_second, conv_image, norm_gain, norm_bias,
):
    images, rows, width, channels = latents.shape
    ndp = lax.axis_size("dp")
    nslab = lax.axis_size("slab")
    t_count = width // S
    pixel_scale = 1.0 / math.sqrt(images * ndp * rows * nslab * width)
    blk = 9 * C // ndp
    pad = -(-blk // 16) * 16
    vmem = pl.BlockSpec(memory_space=pltpu.VMEM)
    smem = pl.BlockSpec(memory_space=pltpu.SMEM)
    edge = (rows + 2, t_count + 2, S, C)
    scratch = [
        pltpu.VMEM((width, width), BF16),
        pltpu.VMEM((width, width), BF16),
        pltpu.VMEM((width, C), jnp.int32),
        pltpu.VMEM((rows, width, C), BF16),
        pltpu.VMEM(edge, BF16),
        pltpu.VMEM(edge, BF16),
        pltpu.VMEM((rows + 2, C, width), BF16),
        pltpu.VMEM((rows + 2, C, width), BF16),
        pltpu.VMEM((rows, width, C), BF16),
        pltpu.VMEM((rows, width, C), F32),
        pltpu.VMEM((rows, width, C), F32),
        pltpu.VMEM((rows, width, C), BF16),
        pltpu.VMEM(edge, BF16),
        pltpu.VMEM(edge, BF16),
        pltpu.VMEM((4, 12 * C, 2 * C), BF16),
        pltpu.VMEM((64, 2 * C), F32),
        pltpu.VMEM((64, 2 * C), BF16),
        pltpu.VMEM((width // C, 16 * rows, C), F32),
        pltpu.VMEM((rows + 2, 16, width), BF16),
        pltpu.VMEM((3 * C, 3 * C), F32),
        pltpu.VMEM((9 * C, C), F32),
        pltpu.VMEM((64, 2 * C), F32),
        pltpu.VMEM((4, 8, C), F32),
        pltpu.VMEM((2, 8, C), F32),
        pltpu.VMEM((2, nslab, 8, C), F32),
        pltpu.VMEM((2, ndp, pad, C), BF16),
        pltpu.VMEM((2, ndp, pad, C), BF16),
        pltpu.VMEM((2, pad, C), BF16),
        pltpu.VMEM((2, nslab, pad, C), BF16),
        pltpu.VMEM((48, C), F32),
        pltpu.VMEM((ndp, 48, C), F32),
        pltpu.VMEM((48, C), F32),
        pltpu.VMEM((nslab, 48, C), F32),
        pltpu.SemaphoreType.DMA((5, 2)),
        pltpu.SemaphoreType.DMA((5, 2)),
        pltpu.SemaphoreType.DMA((2, nslab)),
        pltpu.SemaphoreType.DMA((2, nslab)),
        pltpu.SemaphoreType.DMA((3, ndp)),
        pltpu.SemaphoreType.DMA((3, ndp)),
        pltpu.SemaphoreType.DMA((3, nslab)),
        pltpu.SemaphoreType.DMA((3, nslab)),
    ]
    gw1, gw2, gci, gg, gb, gl = pl.pallas_call(
        functools.partial(kernel, ndp, nslab, rows, width, pixel_scale),
        out_shape=(
            jax.ShapeDtypeStruct((blk, C), F32),
            jax.ShapeDtypeStruct((blk, C), F32),
            jax.ShapeDtypeStruct((3, 9 * C), F32),
            jax.ShapeDtypeStruct((1, C), F32),
            jax.ShapeDtypeStruct((1, C), F32),
            jax.ShapeDtypeStruct((rows, width, C), BF16),
        ),
        in_specs=[vmem, vmem, smem, smem, smem, smem, vmem, vmem, vmem, vmem, vmem],
        out_specs=(vmem,) * 6,
        scratch_shapes=scratch,
        compiler_params=pltpu.CompilerParams(
            collective_id=0, has_side_effects=True, vmem_limit_bytes=60 * 2**20
        ),
        cost_estimate=pl.CostEstimate(
            flops=int(1.6e10), bytes_accessed=5 * 2**20, transcendentals=5 * 2**20
        ),
    )(
        latents[0], image_grad[0], heights, widths, buckets, bucket_scale,
        conv_first, conv_second, conv_image, norm_gain[None], norm_bias[None],
    )
    return gw1, gw2, gci, gg[0], gb[0], gl[None]


def solution(mesh):
    placed = (
        P("dp", "slab", None, None),
        P("dp", None, "slab", None),
        P("dp"),
        P("dp"),
        P("dp"),
        P(),
        P(),
        P(),
        P(),
        P(),
        P(),
    )
    return jax.shard_map(
        shards,
        mesh=mesh,
        in_specs=placed,
        out_specs=(P("dp", None), P("dp", None), P(), P(), P(), P("dp", "slab", None, None)),
        check_vma=False,
    )
```

```python
import functools
import math

import jax
import jax.numpy as jnp
from jax import lax
from jax.experimental import pallas as pl
from jax.experimental.pallas import tpu as pltpu
from jax.sharding import PartitionSpec as P

MESH = pl.DeviceIdType.MESH
F32 = jnp.float32
BF16 = jnp.bfloat16
PER_GROUP = 4
NORM_EPS = 1e-06
S = 16
C = 128


def dot(a, b):
    return jnp.dot(a, b, preferred_element_type=F32)


def sigmoid(v):
    return 0.5 * jnp.tanh(0.5 * v) + 0.5


def group_total(v):
    lane = lax.broadcasted_iota(jnp.int32, v.shape, 1)
    v = v + jnp.where(lane % 2 == 0, pltpu.roll(v, C - 1, 1), pltpu.roll(v, 1, 1))
    return v + jnp.where(lane % 4 < 2, pltpu.roll(v, C - 2, 1), pltpu.roll(v, 2, 1))


def kernel(
    ndp, nslab, rows, width, pixel_scale,
    lat_ref, img_ref, h_ref, w_ref, bk_ref, bs_ref, w1_ref, w2_ref, ci_ref, gain_ref, bias_ref,
    out_ref, pack_ref,
    lat, glp, perm, permt, col, latp, act, mid, actt, midt, h1, h2, gs, nact, b2, b1,
    w4, ci4f, ci4, gstage, gimg, acc, flat, imgacc, sums, stat_send, stat_recv,
    send_c, recv_c, send_a, recv_a, send_b, recv_b,
    small_c, small_rc, small_a, small_ra, small_b, small_rb,
    io_sem, halo_s, halo_r, stat_ss, stat_rs, c_ss, c_rs, a_ss, a_rs, b_ss, b_rs,
):
    t_count = width // S
    last = rows + 1
    npair = rows // 2
    blk = (9 * C) // ndp
    nchip = ndp // 2
    dp = lax.axis_index("dp")
    slab = lax.axis_index("slab")
    core = lax.rem(dp, 2)
    chip = dp // 2

    def latents_in(i):
        part = pl.ds(2 * i, 2)
        return pltpu.make_async_copy(lat_ref.at[part], lat.at[part], io_sem.at[0, i])

    def latents_out(i):
        part = pl.ds(2 * i, 2)
        return pltpu.make_async_copy(glp.at[part], out_ref.at[part], io_sem.at[1, i])

    latents_in(0).start()
    latents_in(npair - 1).start()
    lax.fori_loop(1, npair - 1, lambda i, _: (latents_in(i).start(), 0)[1], 0)

    barrier = pltpu.get_barrier_semaphore()

    def greet(axis, me, n):
        def body(off, _):
            pl.semaphore_signal(
                barrier, inc=1, device_id={axis: lax.rem(me + off, n)}, device_id_type=MESH
            )
            return 0
        lax.fori_loop(1, n, body, 0)

    greet("slab", slab, nslab)
    greet("dp", dp, ndp)

    height = h_ref[0]
    limit = w_ref[0]
    count = (height * limit * PER_GROUP).astype(F32)

    def inside(r):
        return col[...] < jnp.where(slab * rows + r < height, limit, 0)

    def loop(lo, hi, body):
        def step(i, _):
            body(i)
            return 0
        lax.fori_loop(lo, hi, step, 0)

    def put(ref, row, a):
        ref[row, 1:t_count + 1] = a.reshape(t_count, S, C)
        sub = lax.broadcasted_iota(jnp.int32, (S, C), 0)
        low = pltpu.roll(a[width - S:].astype(F32), 1, 0)
        ref[row, 0] = jnp.where(sub == 0, 0.0, low).astype(BF16)
        high = pltpu.roll(a[:S].astype(F32), S - 1, 0)
        ref[row, t_count + 1] = jnp.where(sub == S - 1, 0.0, high).astype(BF16)

    def halo(ref, e, d):
        if d == 0:
            src, dst, to = 1, last, lax.rem(slab + nslab - 1, nslab)
        else:
            src, dst, to = last - 1, 0, lax.rem(slab + 1, nslab)
        return pltpu.make_async_remote_copy(
            src_ref=ref.at[src], dst_ref=ref.at[dst],
            send_sem=halo_s.at[e, d], recv_sem=halo_r.at[e, d],
            device_id={"slab": to}, device_id_type=MESH,
        )

    def halo_start(ref, e):
        for d in range(2):
            halo(ref, e, d).start()

    def halo_wait(ref, e):
        for d in range(2):
            halo(ref, e, d).wait()

        @pl.when(slab == 0)
        def _():
            ref[0] = jnp.zeros(ref.shape[1:], ref.dtype)

        @pl.when(slab == nslab - 1)
        def _():
            ref[last] = jnp.zeros(ref.shape[1:], ref.dtype)

    def spread(src_of, recv, ss, rs, e, axis, me, n, target=lambda peer: peer):
        def copy(peer, slot):
            return pltpu.make_async_remote_copy(
                src_ref=src_of(peer), dst_ref=recv.at[slot],
                send_sem=ss.at[e, peer], recv_sem=rs.at[e, slot],
                device_id={axis: target(peer)}, device_id_type=MESH,
            )

        def start():
            def body(off):
                copy(lax.rem(me + off, n), me).start()
            loop(1, n, body)

        def wait():
            def body(off):
                peer = lax.rem(me + off, n)
                copy(peer, peer).wait_recv()
                copy(peer, me).wait_send()
            loop(1, n, body)

        return start, wait

    def to_core(src, recv, e):
        return pltpu.make_async_remote_copy(
            src_ref=src, dst_ref=recv, send_sem=c_ss.at[e], recv_sem=c_rs.at[e],
            device_id={"dp": dp + 1 - 2 * core}, device_id_type=MESH,
        )

    def to_chips(src_of, recv, e):
        return spread(
            src_of, recv, a_ss, a_rs, e, "dp", chip, nchip, lambda peer: 2 * peer + core
        )

    a_i = lax.broadcasted_iota(jnp.int32, (width, width), 0)
    b_i = lax.broadcasted_iota(jnp.int32, (width, width), 1)
    perm[...] = jnp.where((a_i % S) * t_count + a_i // S == b_i, 1.0, 0.0).astype(BF16)
    permt[...] = jnp.where((b_i % S) * t_count + b_i // S == a_i, 1.0, 0.0).astype(BF16)
    j_i = lax.broadcasted_iota(jnp.int32, (width, C), 0)
    col[...] = (j_i % S) * t_count + j_i // S

    def ends(body):
        loop(0, 2, lambda k: body(k * (npair - 1)))

    def stage_input(i):
        latents_in(i).wait()
        x = dot(perm[...], jnp.concatenate([lat[2 * i], lat[2 * i + 1]], axis=1))
        for k in range(2):
            r = 2 * i + k
            v = x[:, k * C:(k + 1) * C]
            latp[r] = v.astype(BF16)
            a = jnp.where(inside(r), v * sigmoid(v), 0.0).astype(BF16)
            put(act, r + 1, a)
            actt[r + 1] = a.T

    ends(stage_input)
    pl.semaphore_wait(barrier, ndp + nslab - 2)
    halo_start(act, 0)
    loop(1, npair - 1, stage_input)

    scale = bs_ref[bk_ref[0]]
    row3 = lax.broadcasted_iota(jnp.int32, (3, rows, width), 1) + slab * rows
    lane3 = lax.broadcasted_iota(jnp.int32, (3, rows, width), 2)
    graded = jnp.where((row3 < height) & (lane3 < limit), img_ref[...].astype(F32) * scale, 0.0)
    graded = graded.reshape(3 * rows, width)
    lane = lax.broadcasted_iota(jnp.int32, (3 * rows, width), 1)
    shifted = [
        jnp.where(lane == width - 1, 0.0, pltpu.roll(graded, width - 1, 1)),
        graded,
        jnp.where(lane == 0, 0.0, pltpu.roll(graded, 1, 1)),
    ]
    stacked = jnp.concatenate([s.astype(BF16) for s in shifted], axis=0)
    gstage[...] = jnp.zeros_like(gstage)
    placed = dot(stacked, permt[...])
    for k in range(width // C):
        gstage[k, 0:9 * rows] = placed[:, k * C:(k + 1) * C]
        for r in range(rows):
            gimg[r + 1, :, k * C:(k + 1) * C] = gstage[k, pl.ds(r, 16, stride=rows), :].astype(BF16)

    halo_start(gimg, 1)

    for c, (ref, flip) in enumerate(((w1_ref, False), (w2_ref, False), (w2_ref, True), (w1_ref, True))):
        for j in range(4):
            for q in range(3):
                at = (j * 3 + q) * C
                for k in range(2):
                    if 0 <= j - k <= 2:
                        tap = 3 * (j - k) + q
                        if flip:
                            b = ref[(8 - tap) * C:(9 - tap) * C, :].T
                        else:
                            b = ref[tap * C:(tap + 1) * C, :]
                    else:
                        b = jnp.zeros((C, C), BF16)
                    w4[c, at:at + C, k * C:(k + 1) * C] = b
    ci4f[...] = jnp.zeros_like(ci4f)
    for p in range(3):
        for q in range(3):
            piece = ci_ref[:, (3 * p + q) * C:(3 * p + q + 1) * C].astype(F32)
            for k in range(2):
                at = (2 - p + k) * 16 + q * 3
                ci4f[at:at + 3, k * C:(k + 1) * C] = piece
    ci4[...] = ci4f[...].astype(BF16)

    def conv(src, c, i):
        taps = [
            src[2 * i + j, q:q + t_count].reshape(width, C) for j in range(4) for q in range(3)
        ]
        return dot(jnp.concatenate(taps, axis=1), w4[c])

    def stage_one(i):
        y = conv(act, 0, i)
        for k in range(2):
            r = 2 * i + k
            hb = y[:, k * C:(k + 1) * C].astype(BF16)
            h1[r] = hb
            hf = hb.astype(F32)
            m = jnp.where(inside(r), hf * sigmoid(hf), 0.0).astype(BF16)
            put(mid, r + 1, m)
            midt[r + 1] = m.T

    loop(1, npair // 2, stage_one)
    halo_wait(act, 0)
    ends(stage_one)
    halo_start(mid, 2)
    loop(npair // 2, npair - 1, stage_one)
    for e in (0, last):
        actt[e] = act[e, 1:t_count + 1].reshape(width, C).T

    sums[...] = jnp.zeros_like(sums)

    def fold(v):
        return jnp.sum(v.reshape(width // 8, 8, C), axis=0)

    def stage_two(i):
        y = conv(mid, 1, i)
        for k in range(2):
            r = 2 * i + k
            v = y[:, k * C:(k + 1) * C] + latp[r].astype(F32)
            h2[r] = v
            masked = jnp.where(inside(r), v, 0.0)
            sums[0] += fold(masked)
            sums[1] += fold(masked * v)

    loop(1, npair - 1, stage_two)
    halo_wait(mid, 2)
    ends(stage_two)

    def stats(e):
        stat_send[e, 0:1] = jnp.sum(sums[2 * e], axis=0, keepdims=True)
        stat_send[e, 1:2] = jnp.sum(sums[2 * e + 1], axis=0, keepdims=True)
        stat_recv[e, slab] = stat_send[e]
        return spread(
            lambda peer: stat_send.at[e], stat_recv.at[e], stat_ss, stat_rs, e, "slab", slab, nslab
        )

    def stat_total(e):
        total = stat_recv[e, 0]
        for k in range(1, nslab):
            total = total + stat_recv[e, k]
        return total

    for e in range(2):
        stat_send[e] = jnp.zeros(stat_send.shape[1:], F32)
    start, wait = stats(0)
    start()

    halo_wait(gimg, 1)

    def stage_image(i):
        y = lax.dot_general(
            gimg[pl.ds(2 * i, 4)].reshape(64, width), ci4[...], (((0,), (0,)), ((), ())),
            preferred_element_type=F32,
        )
        for k in range(2):
            gs[2 * i + k] = y[:, k * C:(k + 1) * C]

    loop(0, npair, stage_image)
    for e in (0, last):
        midt[e] = mid[e, 1:t_count + 1].reshape(width, C).T
    wait()

    total = stat_total(0)
    mean = group_total(total[0:1]) / count
    rstd = lax.rsqrt(group_total(total[1:2]) / count - mean * mean + NORM_EPS)
    gain = gain_ref[...]
    bias = bias_ref[...]

    def stage_norm(r):
        n = (h2[r] - mean) * rstd
        v = n * gain + bias
        s = sigmoid(v)
        vs = v * s
        here = inside(r)
        nact[r] = jnp.where(here, vs, 0.0).astype(BF16)
        g = jnp.where(here, gs[r] * (s + vs * (1.0 - s)), 0.0)
        h2[r] = n
        gs[r] = g
        sums[2] += fold(g)
        sums[3] += fold(g * n)

    loop(0, rows, stage_norm)
    start, wait = stats(1)
    start()

    imgacc[...] = jnp.zeros_like(imgacc)

    def stage_imgw(i):
        imgacc[...] += dot(
            gimg[pl.ds(2 * i, 4)].reshape(64, width),
            jnp.concatenate([nact[2 * i], nact[2 * i + 1]], axis=1),
        )

    loop(0, npair, stage_imgw)
    flat[0:48] = imgacc[0:48, 0:C] + imgacc[16:64, C:2 * C]
    flat[9:10] = jnp.sum(sums[3], axis=0, keepdims=True)
    flat[10:11] = jnp.sum(sums[2], axis=0, keepdims=True)
    small_c[...] = flat[0:48].astype(BF16)
    to_core(small_c, small_rc, 0).start()
    wait()

    total = stat_total(1)
    c1 = rstd * gain
    c0 = rstd * (group_total(total[0:1] * gain) / count)
    c2 = rstd * (group_total(total[1:2] * gain) / count)

    def stage_grad_two(r):
        g = jnp.where(inside(r), gs[r] * c1 - c0 - h2[r] * c2, 0.0).astype(BF16)
        put(b2, r + 1, g)

    loop(0, 2, lambda k: stage_grad_two(k * (rows - 1)))
    halo_start(b2, 3)
    loop(1, rows - 1, stage_grad_two)

    def weight_grad(at, b):
        acc[...] = jnp.zeros_like(acc)

        def piece(row, q):
            return b[row, 2 - q:2 - q + t_count].reshape(width, C)

        def body(i):
            lhs = jnp.concatenate(
                [at[pl.ds(2 * i + k, 3)].reshape(3 * C, width) for k in range(2)], axis=1
            )
            rhs = jnp.concatenate(
                [
                    jnp.concatenate([piece(2 * i + 1 + k, q) for q in range(2)], axis=1)
                    for k in range(2)
                ],
                axis=0,
            )
            acc[:, 0:2 * C] += dot(lhs, rhs)
            rhs = jnp.concatenate([piece(2 * i + 1 + k, 2) for k in range(2)], axis=1)
            z = dot(at[pl.ds(2 * i, 4)].reshape(4 * C, width), rhs)
            acc[:, 2 * C:] += z[0:3 * C, 0:C] + z[C:, C:]

        loop(0, npair, body)

    def scatter(e):
        for p in range(3):
            for q in range(3):
                flat[(3 * p + q) * C:(3 * p + q + 1) * C] = acc[p * C:(p + 1) * C, q * C:(q + 1) * C]

        def body(d):
            send_c[e, lax.rem(d, 2), d // 2, 0:blk] = flat[
                pl.ds(pl.multiple_of(d * blk, 8), blk)
            ].astype(BF16)
        loop(0, ndp, body)
        copy = to_core(send_c.at[e, 1 - core], recv_c.at[e], 1 + e)
        copy.start()
        return copy

    def chips(e):
        def body(k):
            both = send_c[e, core, k].astype(F32) + recv_c[e, k].astype(F32)
            send_a[e, k] = both.astype(BF16)
        loop(0, nchip, body)
        recv_a[e, chip] = send_a[e, chip]
        start, wait = to_chips(lambda peer: send_a.at[e, peer], recv_a.at[e], 1 + e)
        start()
        return wait

    def gather(e):
        part = recv_a[e, 0].astype(F32)
        for k in range(1, nchip):
            part = part + recv_a[e, k].astype(F32)
        send_b[e] = part.astype(BF16)
        recv_b[e, slab] = send_b[e]
        start, wait = spread(
            lambda peer: send_b.at[e], recv_b.at[e], b_ss, b_rs, 1 + e, "slab", slab, nslab
        )
        start()
        return wait

    def finish(e):
        part = recv_b[e, 0].astype(F32)
        for k in range(1, nslab):
            part = part + recv_b[e, k].astype(F32)
        pack_ref[e * blk:(e + 1) * blk] = part[0:blk] * pixel_scale

    send_c[...] = jnp.zeros_like(send_c)
    weight_grad(midt, b2)
    second = scatter(0)

    to_core(small_c, small_rc, 0).wait()
    small_a[...] = (small_c[...].astype(F32) + small_rc[...].astype(F32)).astype(BF16)
    small_ra[chip] = small_a[...]
    small_start, small_wait = to_chips(lambda peer: small_a, small_ra, 0)
    small_start()

    halo_wait(b2, 3)

    def stage_grad_one(i):
        y = conv(b2, 2, i)
        for k in range(2):
            r = 2 * i + k
            v = h1[r].astype(F32)
            s = sigmoid(v)
            slope = s + v * s * (1.0 - s)
            g = jnp.where(inside(r), y[:, k * C:(k + 1) * C] * slope, 0.0).astype(BF16)
            put(b1, r + 1, g)

    ends(stage_grad_one)
    halo_start(b1, 4)
    second.wait()
    second_wait = chips(0)
    loop(1, npair - 1, stage_grad_one)

    small_wait()
    part = small_ra[0].astype(F32)
    for k in range(1, nchip):
        part = part + small_ra[k].astype(F32)
    small_b[...] = part.astype(BF16)
    small_rb[slab] = small_b[...]
    small_b_start, small_b_wait = spread(
        lambda peer: small_b, small_rb, b_ss, b_rs, 0, "slab", slab, nslab
    )
    small_b_start()
    second_wait()
    second_b_wait = gather(0)

    weight_grad(actt, b1)
    first = scatter(1)
    halo_wait(b1, 4)

    def stage_latents(i):
        y = conv(b1, 3, i)
        for k in range(2):
            r = 2 * i + k
            v = latp[r].astype(F32)
            s = sigmoid(v)
            slope = s + v * s * (1.0 - s)
            g = jnp.where(inside(r), y[:, k * C:(k + 1) * C] * slope, 0.0)
            own = b2[r + 1, 1:t_count + 1].reshape(width, C).astype(F32)
            glp[r] = (own + g).astype(BF16)
        latents_out(i).start()

    loop(0, npair // 4, stage_latents)
    first.wait()
    first_wait = chips(1)
    loop(npair // 4, npair * 5 // 8, stage_latents)
    first_wait()
    first_b_wait = gather(1)
    loop(npair * 5 // 8, npair, stage_latents)

    small_b_wait()
    part = small_rb[0].astype(F32)
    for k in range(1, nslab):
        part = part + small_rb[k].astype(F32)
    pack_ref[2 * blk:2 * blk + 48] = part * pixel_scale
    second_b_wait()
    finish(0)
    first_b_wait()
    finish(1)
    loop(0, npair, lambda i: latents_out(i).wait())


def unload(blk, step_rows, width, glp_ref, pack_ref, gw1_ref, gw2_ref, gci_ref, gg_ref, gb_ref, gl_ref, permt):
    t_count = width // S

    @pl.when(pl.program_id(0) == 0)
    def _():
        a_i = lax.broadcasted_iota(jnp.int32, (width, width), 0)
        b_i = lax.broadcasted_iota(jnp.int32, (width, width), 1)
        permt[...] = jnp.where((b_i % S) * t_count + b_i // S == a_i, 1.0, 0.0).astype(BF16)
        gw1_ref[...] = pack_ref[blk:2 * blk]
        gw2_ref[...] = pack_ref[0:blk]
        base = 2 * blk
        gg_ref[...] = pack_ref[base + 9:base + 10]
        gb_ref[...] = pack_ref[base + 10:base + 11]
        for p in range(3):
            for q in range(3):
                at = base + (2 - p) * 16 + q * 3
                gci_ref[:, (3 * p + q) * C:(3 * p + q + 1) * C] = pack_ref[at:at + 3]

    for i in range(step_rows // 2):
        z = dot(permt[...], jnp.concatenate([glp_ref[2 * i], glp_ref[2 * i + 1]], axis=1))
        for k in range(2):
            gl_ref[2 * i + k] = z[:, k * C:(k + 1) * C].astype(BF16)


def shards(
    latents, image_grad, heights, widths, buckets, bucket_scale,
    conv_first, conv_second, conv_image, norm_gain, norm_bias,
):
    images, rows, width, channels = latents.shape
    ndp = lax.axis_size("dp")
    nslab = lax.axis_size("slab")
    t_count = width // S
    pixel_scale = 1.0 / math.sqrt(images * ndp * rows * nslab * width)
    blk = 9 * C // ndp
    pad = -(-blk // 16) * 16
    vmem = pl.BlockSpec(memory_space=pltpu.VMEM)
    smem = pl.BlockSpec(memory_space=pltpu.SMEM)
    nchip = ndp // 2
    edge = (rows + 2, t_count + 2, S, C)
    scratch = [
        pltpu.VMEM((rows, width, C), BF16),
        pltpu.VMEM((rows, width, C), BF16),
        pltpu.VMEM((width, width), BF16),
        pltpu.VMEM((width, width), BF16),
        pltpu.VMEM((width, C), jnp.int32),
        pltpu.VMEM((rows, width, C), BF16),
        pltpu.VMEM(edge, BF16),
        pltpu.VMEM(edge, BF16),
        pltpu.VMEM((rows + 2, C, width), BF16),
        pltpu.VMEM((rows + 2, C, width), BF16),
        pltpu.VMEM((rows, width, C), BF16),
        pltpu.VMEM((rows, width, C), F32),
        pltpu.VMEM((rows, width, C), F32),
        pltpu.VMEM((rows, width, C), BF16),
        pltpu.VMEM(edge, BF16),
        pltpu.VMEM(edge, BF16),
        pltpu.VMEM((4, 12 * C, 2 * C), BF16),
        pltpu.VMEM((64, 2 * C), F32),
        pltpu.VMEM((64, 2 * C), BF16),
        pltpu.VMEM((width // C, 16 * rows, C), F32),
        pltpu.VMEM((rows + 2, 16, width), BF16),
        pltpu.VMEM((3 * C, 3 * C), F32),
        pltpu.VMEM((9 * C, C), F32),
        pltpu.VMEM((64, 2 * C), F32),
        pltpu.VMEM((4, 8, C), F32),
        pltpu.VMEM((2, 8, C), F32),
        pltpu.VMEM((2, nslab, 8, C), F32),
        pltpu.VMEM((2, 2, nchip, pad, C), BF16),
        pltpu.VMEM((2, nchip, pad, C), BF16),
        pltpu.VMEM((2, nchip, pad, C), BF16),
        pltpu.VMEM((2, nchip, pad, C), BF16),
        pltpu.VMEM((2, pad, C), BF16),
        pltpu.VMEM((2, nslab, pad, C), BF16),
        pltpu.VMEM((48, C), BF16),
        pltpu.VMEM((48, C), BF16),
        pltpu.VMEM((48, C), BF16),
        pltpu.VMEM((nchip, 48, C), BF16),
        pltpu.VMEM((48, C), BF16),
        pltpu.VMEM((nslab, 48, C), BF16),
        pltpu.SemaphoreType.DMA((2, rows // 2)),
        pltpu.SemaphoreType.DMA((5, 2)),
        pltpu.SemaphoreType.DMA((5, 2)),
        pltpu.SemaphoreType.DMA((2, nslab)),
        pltpu.SemaphoreType.DMA((2, nslab)),
        pltpu.SemaphoreType.DMA((3,)),
        pltpu.SemaphoreType.DMA((3,)),
        pltpu.SemaphoreType.DMA((3, nchip)),
        pltpu.SemaphoreType.DMA((3, nchip)),
        pltpu.SemaphoreType.DMA((3, nslab)),
        pltpu.SemaphoreType.DMA((3, nslab)),
    ]
    anywhere = pl.BlockSpec(memory_space=pl.ANY)
    glp, pack = pl.pallas_call(
        functools.partial(kernel, ndp, nslab, rows, width, pixel_scale),
        out_shape=(
            jax.ShapeDtypeStruct((rows, width, C), BF16),
            jax.ShapeDtypeStruct((2 * blk + 48, C), F32),
        ),
        in_specs=[anywhere, vmem, smem, smem, smem, smem, vmem, vmem, vmem, vmem, vmem],
        out_specs=(anywhere, vmem),
        scratch_shapes=scratch,
        compiler_params=pltpu.CompilerParams(
            collective_id=0, has_side_effects=True, vmem_limit_bytes=60 * 2**20
        ),
        cost_estimate=pl.CostEstimate(
            flops=int(1.6e10), bytes_accessed=5 * 2**20, transcendentals=5 * 2**20
        ),
    )(
        latents[0], image_grad[0], heights, widths, buckets, bucket_scale,
        conv_first, conv_second, conv_image, norm_gain[None], norm_bias[None],
    )
    step_rows = 4
    gw1, gw2, gci, gg, gb, gl = pl.pallas_call(
        functools.partial(unload, blk, step_rows, width),
        grid=(rows // step_rows,),
        out_shape=(
            jax.ShapeDtypeStruct((blk, C), F32),
            jax.ShapeDtypeStruct((blk, C), F32),
            jax.ShapeDtypeStruct((3, 9 * C), F32),
            jax.ShapeDtypeStruct((1, C), F32),
            jax.ShapeDtypeStruct((1, C), F32),
            jax.ShapeDtypeStruct((rows, width, C), BF16),
        ),
        in_specs=[
            pl.BlockSpec((step_rows, width, C), lambda i: (i, 0, 0)),
            pl.BlockSpec((2 * blk + 48, C), lambda i: (0, 0)),
        ],
        out_specs=(
            pl.BlockSpec((blk, C), lambda i: (0, 0)),
            pl.BlockSpec((blk, C), lambda i: (0, 0)),
            pl.BlockSpec((3, 9 * C), lambda i: (0, 0)),
            pl.BlockSpec((1, C), lambda i: (0, 0)),
            pl.BlockSpec((1, C), lambda i: (0, 0)),
            pl.BlockSpec((step_rows, width, C), lambda i: (i, 0, 0)),
        ),
        scratch_shapes=[pltpu.VMEM((width, width), BF16)],
        compiler_params=pltpu.CompilerParams(vmem_limit_bytes=16 * 2**20),
    )(glp, pack)
    return gw1, gw2, gci, gg[0], gb[0], gl[None]


def solution(mesh):
    placed = (
        P("dp", "slab", None, None),
        P("dp", None, "slab", None),
        P("dp"),
        P("dp"),
        P("dp"),
        P(),
        P(),
        P(),
        P(),
        P(),
        P(),
    )
    return jax.shard_map(
        shards,
        mesh=mesh,
        in_specs=placed,
        out_specs=(P("dp", None), P("dp", None), P(), P(), P(), P("dp", "slab", None, None)),
        check_vma=False,
    )
```

```python
import functools
import math

import jax
import jax.numpy as jnp
from jax import lax
from jax.experimental import pallas as pl
from jax.experimental.pallas import tpu as pltpu
from jax.sharding import PartitionSpec as P

MESH = pl.DeviceIdType.MESH
F32 = jnp.float32
BF16 = jnp.bfloat16
PER_GROUP = 4
NORM_EPS = 1e-06
S = 16
C = 128


def dot(a, b):
    return jnp.dot(a, b, preferred_element_type=F32)


def sigmoid(v):
    return 0.5 * jnp.tanh(0.5 * v) + 0.5


def group_total(v):
    lane = lax.broadcasted_iota(jnp.int32, v.shape, 1)
    v = v + jnp.where(lane % 2 == 0, pltpu.roll(v, C - 1, 1), pltpu.roll(v, 1, 1))
    return v + jnp.where(lane % 4 < 2, pltpu.roll(v, C - 2, 1), pltpu.roll(v, 2, 1))


def kernel(
    ndp, nslab, rows, width, pixel_scale,
    lat_ref, img_ref, h_ref, w_ref, bk_ref, bs_ref, w1_ref, w2_ref, ci_ref, gain_ref, bias_ref,
    out_ref, gw_ref, gci_ref, gn_ref,
    lat, lath, glp, slope0, slope1, perm, permt, col, latp, act, mid, actt, midt, h1, h2, gs, nact, b2, b1,
    wi, wo, ci4f, ci4, gstage, gimg, acc, flat, imgacc, sums, stat_send, stat_recv,
    send_c, recv_c, send_a, recv_a, send_b, recv_b,
    small_c, small_rc, small_a, small_ra, small_b, small_rb,
    io_sem, halo_s, halo_r, stat_ss, stat_rs, c_ss, c_rs, a_ss, a_rs, b_ss, b_rs,
):
    t_count = width // S
    last = rows + 1
    npair = rows // 2
    blk = (9 * C) // ndp
    nchip = ndp // 2
    dp = lax.axis_index("dp")
    slab = lax.axis_index("slab")
    core = lax.rem(dp, 2)
    chip = dp // 2

    def latents_in(i):
        part = pl.ds(2 * i, 2)
        return pltpu.make_async_copy(lat_ref.at[part], lat.at[part], io_sem.at[0, i])

    def latents_out(i):
        part = pl.ds(2 * i, 2)
        return pltpu.make_async_copy(glp.at[part], out_ref.at[part], io_sem.at[1, i])

    latents_in(0).start()
    latents_in(npair - 1).start()
    lax.fori_loop(1, npair - 1, lambda i, _: (latents_in(i).start(), 0)[1], 0)

    barrier = pltpu.get_barrier_semaphore()

    def greet(axis, me, n):
        def body(off, _):
            pl.semaphore_signal(
                barrier, inc=1, device_id={axis: lax.rem(me + off, n)}, device_id_type=MESH
            )
            return 0
        lax.fori_loop(1, n, body, 0)

    greet("slab", slab, nslab)
    greet("dp", dp, ndp)

    height = h_ref[0]
    limit = w_ref[0]
    count = (height * limit * PER_GROUP).astype(F32)

    def inside(r):
        at = slab * rows + r
        return col[...] < jnp.where((at >= 0) & (at < height), limit, 0)

    def loop(lo, hi, body, unroll=1):
        if hi - lo <= unroll:
            for i in range(lo, hi):
                body(i)
            return
        assert (hi - lo) % unroll == 0

        def step(i, _):
            for k in range(unroll):
                body(lo + i * unroll + k)
            return 0
        lax.fori_loop(0, (hi - lo) // unroll, step, 0)

    def put(ref, row, a):
        ref[row, 1:t_count + 1] = a.reshape(t_count, S, C)
        sub = lax.broadcasted_iota(jnp.int32, (S, C), 0)
        low = pltpu.roll(a[width - S:].astype(F32), 1, 0)
        ref[row, 0] = jnp.where(sub == 0, 0.0, low).astype(BF16)
        high = pltpu.roll(a[:S].astype(F32), S - 1, 0)
        ref[row, t_count + 1] = jnp.where(sub == S - 1, 0.0, high).astype(BF16)

    def neighbour(src, dst, e, d):
        to = lax.rem(slab + (1 if d else nslab - 1), nslab)
        return pltpu.make_async_remote_copy(
            src_ref=src, dst_ref=dst, send_sem=halo_s.at[e, d], recv_sem=halo_r.at[e, d],
            device_id={"slab": to}, device_id_type=MESH,
        )

    def halo(ref, e, d):
        src, dst = (last - 1, 0) if d else (1, last)
        return neighbour(ref.at[src], ref.at[dst], e, d)

    def latent_halo(d):
        src = lat_ref.at[pl.ds(rows - 2 if d else 0, 2)]
        return neighbour(src, lath.at[1 - d], 0, d)

    def halo_start(ref, e):
        for d in range(2):
            halo(ref, e, d).start()

    def halo_wait(ref, e):
        for d in range(2):
            halo(ref, e, d).wait()

        @pl.when(slab == 0)
        def _():
            ref[0] = jnp.zeros(ref.shape[1:], ref.dtype)

        @pl.when(slab == nslab - 1)
        def _():
            ref[last] = jnp.zeros(ref.shape[1:], ref.dtype)

    def spread(src_of, recv, ss, rs, e, axis, me, n, target=lambda peer: peer):
        def copy(peer, slot):
            return pltpu.make_async_remote_copy(
                src_ref=src_of(peer), dst_ref=recv.at[slot],
                send_sem=ss.at[e, peer], recv_sem=rs.at[e, slot],
                device_id={axis: target(peer)}, device_id_type=MESH,
            )

        def start():
            def body(off):
                copy(lax.rem(me + off, n), me).start()
            loop(1, n, body)

        def wait():
            def body(off):
                peer = lax.rem(me + off, n)
                copy(peer, peer).wait_recv()
                copy(peer, me).wait_send()
            loop(1, n, body)

        return start, wait

    def to_core(src, recv, e):
        return pltpu.make_async_remote_copy(
            src_ref=src, dst_ref=recv, send_sem=c_ss.at[e], recv_sem=c_rs.at[e],
            device_id={"dp": dp + 1 - 2 * core}, device_id_type=MESH,
        )

    def to_chips(src_of, recv, e):
        return spread(
            src_of, recv, a_ss, a_rs, e, "dp", chip, nchip, lambda peer: 2 * peer + core
        )

    a_i = lax.broadcasted_iota(jnp.int32, (width, width), 0)
    b_i = lax.broadcasted_iota(jnp.int32, (width, width), 1)
    perm[...] = jnp.where((a_i % S) * t_count + a_i // S == b_i, 1.0, 0.0).astype(BF16)
    permt[...] = jnp.where((b_i % S) * t_count + b_i // S == a_i, 1.0, 0.0).astype(BF16)
    j_i = lax.broadcasted_iota(jnp.int32, (width, C), 0)
    col[...] = (j_i % S) * t_count + j_i // S

    def ends(body):
        body(0)
        body(npair - 1)

    def input_rows(r0, pair):
        x = dot(perm[...], jnp.concatenate(pair, axis=1))
        kept = []
        for k in range(2):
            v = x[:, k * C:(k + 1) * C]
            a = jnp.where(inside(r0 + k), v * sigmoid(v), 0.0).astype(BF16)
            put(act, r0 + k + 2, a)
            kept.append(v.astype(BF16))
        return kept

    def stage_input(i):
        latents_in(i).wait()
        kept = input_rows(2 * i, [lat[2 * i], lat[2 * i + 1]])
        for k in range(2):
            latp[2 * i + k] = kept[k]

    pl.semaphore_wait(barrier, ndp + nslab - 2)
    for d in range(2):
        latent_halo(d).start()
    loop(0, npair, stage_input, 4)

    scale = bs_ref[bk_ref[0]]
    row3 = lax.broadcasted_iota(jnp.int32, (3, rows, width), 1) + slab * rows
    lane3 = lax.broadcasted_iota(jnp.int32, (3, rows, width), 2)
    graded = jnp.where((row3 < height) & (lane3 < limit), img_ref[...].astype(F32) * scale, 0.0)
    graded = graded.reshape(3 * rows, width)
    lane = lax.broadcasted_iota(jnp.int32, (3 * rows, width), 1)
    shifted = [
        jnp.where(lane == width - 1, 0.0, pltpu.roll(graded, width - 1, 1)),
        graded,
        jnp.where(lane == 0, 0.0, pltpu.roll(graded, 1, 1)),
    ]
    stacked = jnp.concatenate([s.astype(BF16) for s in shifted], axis=0)
    gstage[...] = jnp.zeros_like(gstage)
    placed = dot(stacked, permt[...])
    for k in range(width // C):
        gstage[k, 0:9 * rows] = placed[:, k * C:(k + 1) * C]
        for r in range(rows):
            gimg[r + 1, :, k * C:(k + 1) * C] = gstage[k, pl.ds(r, 16, stride=rows), :].astype(BF16)

    halo_start(gimg, 1)

    zero = jnp.zeros((C, C), BF16)

    def weights(c, ref, flip):
        def tap(p, q):
            n = 3 * p + q
            return ref[(8 - n) * C:(9 - n) * C, :].T if flip else ref[n * C:(n + 1) * C, :]

        for j in range(1, 3):
            for q in range(3):
                at = (3 * (j - 1) + q) * C
                for k in range(2):
                    wi[c, at:at + C, k * C:(k + 1) * C] = tap(j - k, q)
        for k in range(2):
            wo[c, k, 0:C, 0:C] = tap(2 * k, 0)
            wo[c, k, 0:C, C:] = zero
            wo[c, k, C:, 0:C] = tap(2 * k, 1)
            wo[c, k, C:, C:] = tap(2 * k, 2)

    weights(0, w1_ref, False)
    weights(1, w2_ref, False)
    ci4f[...] = jnp.zeros_like(ci4f)
    for p in range(3):
        for q in range(3):
            piece = ci_ref[:, (3 * p + q) * C:(3 * p + q + 1) * C].astype(F32)
            for k in range(2):
                at = (2 - p + k) * 16 + q * 3
                ci4f[at:at + 3, k * C:(k + 1) * C] = piece
    ci4[...] = ci4f[...].astype(BF16)

    def conv(src, c, i):
        taps = [
            src[2 * i + j, q:q + t_count].reshape(width, C) for j in (1, 2) for q in range(3)
        ]
        inner = dot(jnp.concatenate(taps, axis=1), wi[c])
        done = []
        for k in range(2):
            pair = [
                src[2 * i + 3 * k, q:q + t_count + 1].reshape(width + S, C) for q in range(2)
            ]
            outer = dot(jnp.concatenate(pair, axis=1), wo[c, k])
            done.append(inner[:, k * C:(k + 1) * C] + outer[0:width, 0:C] + outer[S:, C:])
        return done

    def stage_one(i):
        y = conv(act, 0, i)
        for k in range(2):
            hb = y[k].astype(BF16)
            h1[2 * i + k] = hb
            hf = hb.astype(F32)
            m = jnp.where(inside(2 * i - 1 + k), hf * sigmoid(hf), 0.0).astype(BF16)
            put(mid, 2 * i + k, m)

    loop(1, npair, stage_one, npair - 1)

    sums[...] = jnp.zeros_like(sums)

    def fold(v):
        return jnp.sum(v.reshape(width // 8, 8, C), axis=0)

    def stage_two(i):
        y = conv(mid, 1, i)
        for k in range(2):
            r = 2 * i + k
            v = y[k] + latp[r].astype(F32)
            h2[r] = v
            masked = jnp.where(inside(r), v, 0.0)
            sums[0] += fold(masked)
            sums[1] += fold(masked * v)

    loop(1, npair - 1, stage_two, 3)

    for d in range(2):
        latent_halo(d).wait()
    input_rows(-2, [lath[0, 0], lath[0, 1]])
    input_rows(rows, [lath[1, 0], lath[1, 1]])
    stage_one(0)
    stage_one(npair)
    ends(stage_two)

    def stats(e):
        stat_send[e, 0:1] = jnp.sum(sums[2 * e], axis=0, keepdims=True)
        stat_send[e, 1:2] = jnp.sum(sums[2 * e + 1], axis=0, keepdims=True)
        stat_recv[e, slab] = stat_send[e]
        return spread(
            lambda peer: stat_send.at[e], stat_recv.at[e], stat_ss, stat_rs, e, "slab", slab, nslab
        )

    def stat_total(e):
        total = stat_recv[e, 0]
        for k in range(1, nslab):
            total = total + stat_recv[e, k]
        return total

    for e in range(2):
        stat_send[e] = jnp.zeros(stat_send.shape[1:], F32)
    start, wait = stats(0)
    start()

    halo_wait(gimg, 1)

    def stage_image(i):
        y = lax.dot_general(
            gimg[pl.ds(2 * i, 4)].reshape(64, width), ci4[...], (((0,), (0,)), ((), ())),
            preferred_element_type=F32,
        )
        for k in range(2):
            gs[2 * i + k] = jnp.where(inside(2 * i + k), y[:, k * C:(k + 1) * C], 0.0)

    loop(0, npair, stage_image, 4)
    weights(2, w2_ref, True)
    weights(3, w1_ref, True)

    def stage_slopes(r):
        here = inside(r)
        for kept, out in ((h1[r + 1], slope1), (latp[r], slope0)):
            v = kept.astype(F32)
            t = sigmoid(v)
            out[r] = jnp.where(here, t + v * t * (1.0 - t), 0.0)

    loop(0, rows, stage_slopes)
    wait()

    total = stat_total(0)
    mean = group_total(total[0:1]) / count
    rstd = lax.rsqrt(group_total(total[1:2]) / count - mean * mean + NORM_EPS)
    gain = gain_ref[...]
    bias = bias_ref[...]

    c1 = rstd * gain

    def stage_norm(r):
        centred = h2[r] - mean
        v = centred * c1 + bias
        s = sigmoid(v)
        vs = v * s
        nact[r] = jnp.where(inside(r), vs, 0.0).astype(BF16)
        g = gs[r] * (s + vs * (1.0 - s))
        gs[r] = g
        sums[2] += fold(g)
        sums[3] += fold(g * centred)

    loop(0, rows, stage_norm)
    start, wait = stats(1)
    start()

    imgacc[...] = jnp.zeros_like(imgacc)

    def stage_imgw(i):
        imgacc[...] += dot(
            gimg[pl.ds(2 * i, 4)].reshape(64, width),
            jnp.concatenate([nact[2 * i], nact[2 * i + 1]], axis=1),
        )

    loop(0, npair, stage_imgw, 4)
    flat[0:48] = imgacc[0:48, 0:C] + imgacc[16:64, C:2 * C]
    flat[9:10] = jnp.sum(sums[3], axis=0, keepdims=True) * rstd
    flat[10:11] = jnp.sum(sums[2], axis=0, keepdims=True)
    small_c[...] = flat[0:48].astype(BF16)
    to_core(small_c, small_rc, 0).start()

    def transposed(src, off, dst):
        def body(row):
            dst[row] = src[row + off, 1:t_count + 1].reshape(width, C).T
        loop(0, last + 1, body, 3)

    transposed(mid, 0, midt)
    transposed(act, 1, actt)
    wait()

    total = stat_total(1)
    c0 = rstd * (group_total(total[0:1] * gain) / count)
    c2 = rstd * rstd * (rstd * group_total(total[1:2] * gain) / count)

    def stage_grad_two(r):
        g = jnp.where(inside(r), gs[r] * c1 - c0 - (h2[r] - mean) * c2, 0.0).astype(BF16)
        put(b2, r + 1, g)

    stage_grad_two(0)
    stage_grad_two(rows - 1)
    halo_start(b2, 3)
    loop(1, rows - 1, stage_grad_two, 2)

    def weight_grad(at, b):
        acc[...] = jnp.zeros_like(acc)

        def piece(row, q):
            return b[row, 2 - q:2 - q + t_count].reshape(width, C)

        many = min(4, npair)

        def body(i):
            firsts = [2 * (i * many + u) for u in range(many)]
            lhs = jnp.concatenate(
                [at[pl.ds(r + k, 3)].reshape(3 * C, width) for r in firsts for k in range(2)], axis=1
            )
            rhs = jnp.concatenate(
                [
                    jnp.concatenate([piece(r + 1 + k, q) for q in range(2)], axis=1)
                    for r in firsts for k in range(2)
                ],
                axis=0,
            )
            acc[:, 0:2 * C] += dot(lhs, rhs)
            lhs = jnp.concatenate(
                [at[pl.ds(r, 4)].reshape(4 * C, width) for r in firsts], axis=1
            )
            rhs = jnp.concatenate(
                [jnp.concatenate([piece(r + 1 + k, 2) for k in range(2)], axis=1) for r in firsts],
                axis=0,
            )
            z = dot(lhs, rhs)
            acc[:, 2 * C:] += z[0:3 * C, 0:C] + z[C:, C:]

        loop(0, npair // many, body)

    def scatter(e):
        for p in range(3):
            for q in range(3):
                flat[(3 * p + q) * C:(3 * p + q + 1) * C] = acc[p * C:(p + 1) * C, q * C:(q + 1) * C]

        def body(d):
            send_c[e, lax.rem(d, 2), d // 2, 0:blk] = flat[
                pl.ds(pl.multiple_of(d * blk, 8), blk)
            ].astype(BF16)
        loop(0, ndp, body)
        copy = to_core(send_c.at[e, 1 - core], recv_c.at[e], 1 + e)
        copy.start()
        return copy

    def chips(e):
        def body(k):
            both = send_c[e, core, k].astype(F32) + recv_c[e, k].astype(F32)
            send_a[e, k] = both.astype(BF16)
        loop(0, nchip, body)
        recv_a[e, chip] = send_a[e, chip]
        start, wait = to_chips(lambda peer: send_a.at[e, peer], recv_a.at[e], 1 + e)
        start()
        return wait

    def gather(e):
        part = recv_a[e, 0].astype(F32)
        for k in range(1, nchip):
            part = part + recv_a[e, k].astype(F32)
        send_b[e] = part.astype(BF16)
        recv_b[e, slab] = send_b[e]
        start, wait = spread(
            lambda peer: send_b.at[e], recv_b.at[e], b_ss, b_rs, 1 + e, "slab", slab, nslab
        )
        start()
        return wait

    def finish(e):
        part = recv_b[e, 0].astype(F32)
        for k in range(1, nslab):
            part = part + recv_b[e, k].astype(F32)
        gw_ref[1 - e] = part[0:blk] * pixel_scale

    send_c[...] = jnp.zeros_like(send_c)
    weight_grad(midt, b2)
    second = scatter(0)

    to_core(small_c, small_rc, 0).wait()
    small_a[...] = (small_c[...].astype(F32) + small_rc[...].astype(F32)).astype(BF16)
    small_ra[chip] = small_a[...]
    small_start, small_wait = to_chips(lambda peer: small_a, small_ra, 0)
    small_start()

    def stage_grad_one(i):
        y = conv(b2, 2, i)
        for k in range(2):
            r = 2 * i + k
            put(b1, r + 1, (y[k] * slope1[r]).astype(BF16))

    loop(1, npair - 1, stage_grad_one, 3)
    halo_wait(b2, 3)
    ends(stage_grad_one)
    halo_start(b1, 4)
    second.wait()
    second_wait = chips(0)

    weight_grad(actt, b1)
    first = scatter(1)

    def stage_latents(i):
        y = conv(b1, 3, i)
        done = []
        for k in range(2):
            r = 2 * i + k
            g = y[k] * slope0[r]
            own = b2[r + 1, 1:t_count + 1].reshape(width, C).astype(F32)
            done.append((own + g).astype(BF16))
        z = dot(permt[...], jnp.concatenate(done, axis=1)).astype(BF16)
        for k in range(2):
            glp[2 * i + k] = z[:, k * C:(k + 1) * C]
        latents_out(i).start()

    loop(1, 1 + (npair - 2) // 2, stage_latents, 3)
    first.wait()
    first_wait = chips(1)
    small_wait()
    part = small_ra[0].astype(F32)
    for k in range(1, nchip):
        part = part + small_ra[k].astype(F32)
    small_b[...] = part.astype(BF16)
    small_rb[slab] = small_b[...]
    small_b_start, small_b_wait = spread(
        lambda peer: small_b, small_rb, b_ss, b_rs, 0, "slab", slab, nslab
    )
    small_b_start()
    second_wait()
    second_b_wait = gather(0)

    loop(1 + (npair - 2) // 2, npair - 1, stage_latents, 3)
    halo_wait(b1, 4)
    ends(stage_latents)
    first_wait()
    first_b_wait = gather(1)

    small_b_wait()
    part = small_rb[0].astype(F32)
    for k in range(1, nslab):
        part = part + small_rb[k].astype(F32)
    part = part * pixel_scale
    gn_ref[0] = part[9:10]
    gn_ref[1] = part[10:11]
    for p in range(3):
        for q in range(3):
            at = (2 - p) * 16 + q * 3
            gci_ref[:, (3 * p + q) * C:(3 * p + q + 1) * C] = part[at:at + 3]
    second_b_wait()
    finish(0)
    first_b_wait()
    finish(1)
    loop(0, npair, lambda i: latents_out(i).wait())


def unload(parts, gl_in, gw_in, gci_in, gn_in, gw1, gw2, gci, gg, gb, gl, gl_buf, gw_buf, gci_buf, gn_buf, sem):
    step = gl_buf.shape[0] // parts
    moves = [(gw_in.at[0], gw_buf.at[0], gw1), (gw_in.at[1], gw_buf.at[1], gw2), (gci_in, gci_buf, gci)]
    moves += [(gn_in.at[0], gn_buf.at[0], gg), (gn_in.at[1], gn_buf.at[1], gb)]
    for i in range(parts):
        rows = pl.ds(i * step, step)
        moves.append((gl_in.at[rows], gl_buf.at[rows], gl.at[rows]))
    into = [pltpu.make_async_copy(m[0], m[1], sem.at[0, i]) for i, m in enumerate(moves)]
    back = [pltpu.make_async_copy(m[1], m[2], sem.at[1, i]) for i, m in enumerate(moves)]
    order = list(range(5, 5 + parts)) + list(range(5))
    for i in order:
        into[i].start()
    for i in order:
        into[i].wait()
        back[i].start()
    for i in order:
        back[i].wait()


def shards(
    latents, image_grad, heights, widths, buckets, bucket_scale,
    conv_first, conv_second, conv_image, norm_gain, norm_bias,
):
    images, rows, width, channels = latents.shape
    ndp = lax.axis_size("dp")
    nslab = lax.axis_size("slab")
    t_count = width // S
    pixel_scale = 1.0 / math.sqrt(images * ndp * rows * nslab * width)
    blk = 9 * C // ndp
    pad = -(-blk // 16) * 16
    vmem = pl.BlockSpec(memory_space=pltpu.VMEM)
    smem = pl.BlockSpec(memory_space=pltpu.SMEM)
    nchip = ndp // 2
    edge = (rows + 2, t_count + 2, S, C)
    wide = (rows + 4, t_count + 2, S, C)
    scratch = [
        pltpu.VMEM((rows, width, C), BF16),
        pltpu.VMEM((2, 2, width, C), BF16),
        pltpu.VMEM((rows, width, C), BF16),
        pltpu.VMEM((rows, width, C), F32),
        pltpu.VMEM((rows, width, C), F32),
        pltpu.VMEM((width, width), BF16),
        pltpu.VMEM((width, width), BF16),
        pltpu.VMEM((width, C), jnp.int32),
        pltpu.VMEM((rows, width, C), BF16),
        pltpu.VMEM(wide, BF16),
        pltpu.VMEM(edge, BF16),
        pltpu.VMEM((rows + 2, C, width), BF16),
        pltpu.VMEM((rows + 2, C, width), BF16),
        pltpu.VMEM((rows + 2, width, C), BF16),
        pltpu.VMEM((rows, width, C), F32),
        pltpu.VMEM((rows, width, C), F32),
        pltpu.VMEM((rows, width, C), BF16),
        pltpu.VMEM(edge, BF16),
        pltpu.VMEM(edge, BF16),
        pltpu.VMEM((4, 6 * C, 2 * C), BF16),
        pltpu.VMEM((4, 2, 2 * C, 2 * C), BF16),
        pltpu.VMEM((64, 2 * C), F32),
        pltpu.VMEM((64, 2 * C), BF16),
        pltpu.VMEM((width // C, 16 * rows, C), F32),
        pltpu.VMEM((rows + 2, 16, width), BF16),
        pltpu.VMEM((3 * C, 3 * C), F32),
        pltpu.VMEM((9 * C, C), F32),
        pltpu.VMEM((64, 2 * C), F32),
        pltpu.VMEM((4, 8, C), F32),
        pltpu.VMEM((2, 8, C), F32),
        pltpu.VMEM((2, nslab, 8, C), F32),
        pltpu.VMEM((2, 2, nchip, pad, C), BF16),
        pltpu.VMEM((2, nchip, pad, C), BF16),
        pltpu.VMEM((2, nchip, pad, C), BF16),
        pltpu.VMEM((2, nchip, pad, C), BF16),
        pltpu.VMEM((2, pad, C), BF16),
        pltpu.VMEM((2, nslab, pad, C), BF16),
        pltpu.VMEM((48, C), BF16),
        pltpu.VMEM((48, C), BF16),
        pltpu.VMEM((48, C), BF16),
        pltpu.VMEM((nchip, 48, C), BF16),
        pltpu.VMEM((48, C), BF16),
        pltpu.VMEM((nslab, 48, C), BF16),
        pltpu.SemaphoreType.DMA((2, rows // 2)),
        pltpu.SemaphoreType.DMA((5, 2)),
        pltpu.SemaphoreType.DMA((5, 2)),
        pltpu.SemaphoreType.DMA((2, nslab)),
        pltpu.SemaphoreType.DMA((2, nslab)),
        pltpu.SemaphoreType.DMA((3,)),
        pltpu.SemaphoreType.DMA((3,)),
        pltpu.SemaphoreType.DMA((3, nchip)),
        pltpu.SemaphoreType.DMA((3, nchip)),
        pltpu.SemaphoreType.DMA((3, nslab)),
        pltpu.SemaphoreType.DMA((3, nslab)),
    ]
    anywhere = pl.BlockSpec(memory_space=pl.ANY)
    staged = pl.pallas_call(
        functools.partial(kernel, ndp, nslab, rows, width, pixel_scale),
        out_shape=(
            jax.ShapeDtypeStruct((rows, width, C), BF16),
            jax.ShapeDtypeStruct((2, blk, C), F32),
            jax.ShapeDtypeStruct((3, 9 * C), F32),
            jax.ShapeDtypeStruct((2, 1, C), F32),
        ),
        in_specs=[anywhere, vmem, smem, smem, smem, smem, vmem, vmem, vmem, vmem, vmem],
        out_specs=(anywhere, vmem, vmem, vmem),
        scratch_shapes=scratch,
        compiler_params=pltpu.CompilerParams(
            collective_id=0, has_side_effects=True, vmem_limit_bytes=60 * 2**20
        ),
        cost_estimate=pl.CostEstimate(
            flops=int(1.6e10), bytes_accessed=5 * 2**20, transcendentals=5 * 2**20
        ),
    )(
        latents[0], image_grad[0], heights, widths, buckets, bucket_scale,
        conv_first, conv_second, conv_image, norm_gain[None], norm_bias[None],
    )
    parts = 4
    gw1, gw2, gci, gg, gb, gl = pl.pallas_call(
        functools.partial(unload, parts),
        out_shape=(
            jax.ShapeDtypeStruct((blk, C), F32),
            jax.ShapeDtypeStruct((blk, C), F32),
            jax.ShapeDtypeStruct((3, 9 * C), F32),
            jax.ShapeDtypeStruct((1, C), F32),
            jax.ShapeDtypeStruct((1, C), F32),
            jax.ShapeDtypeStruct((rows, width, C), BF16),
        ),
        in_specs=[anywhere] * 4,
        out_specs=(anywhere,) * 6,
        scratch_shapes=[
            pltpu.VMEM((rows, width, C), BF16),
            pltpu.VMEM((2, blk, C), F32),
            pltpu.VMEM((3, 9 * C), F32),
            pltpu.VMEM((2, 1, C), F32),
            pltpu.SemaphoreType.DMA((2, parts + 5)),
        ],
        compiler_params=pltpu.CompilerParams(vmem_limit_bytes=60 * 2**20),
    )(*staged)
    return gw1, gw2, gci, gg[0], gb[0], gl[None]


def solution(mesh):
    placed = (
        P("dp", "slab", None, None),
        P("dp", None, "slab", None),
        P("dp"),
        P("dp"),
        P("dp"),
        P(),
        P(),
        P(),
        P(),
        P(),
        P(),
    )
    return jax.shard_map(
        shards,
        mesh=mesh,
        in_specs=placed,
        out_specs=(P("dp", None), P("dp", None), P(), P(), P(), P("dp", "slab", None, None)),
        check_vma=False,
    )
```

```python
import functools
import math

import jax
import jax.numpy as jnp
from jax import lax
from jax.experimental import pallas as pl
from jax.experimental.pallas import tpu as pltpu
from jax.sharding import PartitionSpec as P

MESH = pl.DeviceIdType.MESH
F32 = jnp.float32
BF16 = jnp.bfloat16
PER_GROUP = 4
NORM_EPS = 1e-06
S = 16
C = 128


def dot(a, b):
    return jnp.dot(a, b, preferred_element_type=F32)


def sigmoid(v):
    return 0.5 * jnp.tanh(0.5 * v) + 0.5


def group_total(v):
    lane = lax.broadcasted_iota(jnp.int32, v.shape, 1)
    v = v + jnp.where(lane % 2 == 0, pltpu.roll(v, C - 1, 1), pltpu.roll(v, 1, 1))
    return v + jnp.where(lane % 4 < 2, pltpu.roll(v, C - 2, 1), pltpu.roll(v, 2, 1))


def kernel(
    ndp, nslab, rows, width, pixel_scale,
    lat_ref, img_in, h_ref, w_ref, bk_ref, bs_ref, w1_in, w2_in, ci_ref, gain_ref, bias_ref,
    out_ref, gw_ref, gci_ref, gn_ref,
    img_ref, w1_ref, w2_ref, load_sem, lat, lath, glp, slope0, slope1, perm, permt, col, latp, act, mid, actt, midt, h1, h2, gs, nact, b2, b1,
    wi, wo, ci4f, ci4, gstage, gimg, acc, flat, imgacc, sums, stat_send, stat_recv,
    send_c, recv_c, send_a, recv_a, send_b, recv_b,
    small_c, small_rc, small_a, small_ra, small_b, small_rb,
    io_sem, halo_s, halo_r, stat_ss, stat_rs, c_ss, c_rs, a_ss, a_rs, b_ss, b_rs,
):
    t_count = width // S
    last = rows + 1
    npair = rows // 2
    blk = (9 * C) // ndp
    nchip = ndp // 2
    dp = lax.axis_index("dp")
    slab = lax.axis_index("slab")
    core = lax.rem(dp, 2)
    chip = dp // 2

    def latents_in(i):
        part = pl.ds(2 * i, 2)
        return pltpu.make_async_copy(lat_ref.at[part], lat.at[part], io_sem.at[0, i])

    def latents_out(i):
        part = pl.ds(2 * i, 2)
        return pltpu.make_async_copy(glp.at[part], out_ref.at[part], io_sem.at[1, i])

    lax.fori_loop(0, npair, lambda i, _: (latents_in(i).start(), 0)[1], 0)
    loads = [
        pltpu.make_async_copy(src, dst, load_sem.at[i])
        for i, (src, dst) in enumerate(((img_in, img_ref), (w1_in, w1_ref), (w2_in, w2_ref)))
    ]
    for copy in loads:
        copy.start()

    barrier = pltpu.get_barrier_semaphore()

    def greet(axis, me, n):
        def body(off, _):
            pl.semaphore_signal(
                barrier, inc=1, device_id={axis: lax.rem(me + off, n)}, device_id_type=MESH
            )
            return 0
        lax.fori_loop(1, n, body, 0)

    greet("slab", slab, nslab)
    greet("dp", dp, ndp)

    height = h_ref[0]
    limit = w_ref[0]
    count = (height * limit * PER_GROUP).astype(F32)

    def inside(r):
        at = slab * rows + r
        return col[...] < jnp.where((at >= 0) & (at < height), limit, 0)

    def loop(lo, hi, body, unroll=1):
        if hi - lo <= unroll:
            for i in range(lo, hi):
                body(i)
            return
        assert (hi - lo) % unroll == 0

        def step(i, _):
            for k in range(unroll):
                body(lo + i * unroll + k)
            return 0
        lax.fori_loop(0, (hi - lo) // unroll, step, 0)

    def put(ref, row, a):
        ref[row, 1:t_count + 1] = a.reshape(t_count, S, C)
        sub = lax.broadcasted_iota(jnp.int32, (S, C), 0)
        low = pltpu.roll(a[width - S:].astype(F32), 1, 0)
        ref[row, 0] = jnp.where(sub == 0, 0.0, low).astype(BF16)
        high = pltpu.roll(a[:S].astype(F32), S - 1, 0)
        ref[row, t_count + 1] = jnp.where(sub == S - 1, 0.0, high).astype(BF16)

    def neighbour(src, dst, e, d):
        to = lax.rem(slab + (1 if d else nslab - 1), nslab)
        return pltpu.make_async_remote_copy(
            src_ref=src, dst_ref=dst, send_sem=halo_s.at[e, d], recv_sem=halo_r.at[e, d],
            device_id={"slab": to}, device_id_type=MESH,
        )

    def halo(ref, e, d):
        src, dst = (last - 1, 0) if d else (1, last)
        return neighbour(ref.at[src], ref.at[dst], e, d)

    def latent_halo(d):
        src = lat_ref.at[pl.ds(rows - 2 if d else 0, 2)]
        return neighbour(src, lath.at[1 - d], 0, d)

    above, below = slab > 0, slab < nslab - 1

    def exchange_start(copy):
        @pl.when(above)
        def _():
            copy(0).start()

        @pl.when(below)
        def _():
            copy(1).start()

    def exchange_wait(copy):
        @pl.when(above)
        def _():
            copy(0).wait_send()
            copy(1).wait_recv()

        @pl.when(below)
        def _():
            copy(1).wait_send()
            copy(0).wait_recv()

    def halo_start(ref, e):
        exchange_start(lambda d: halo(ref, e, d))

    def halo_wait(ref, e):
        exchange_wait(lambda d: halo(ref, e, d))

        @pl.when(slab == 0)
        def _():
            ref[0] = jnp.zeros(ref.shape[1:], ref.dtype)

        @pl.when(slab == nslab - 1)
        def _():
            ref[last] = jnp.zeros(ref.shape[1:], ref.dtype)

    def spread(src_of, recv, ss, rs, e, axis, me, n, target=lambda peer: peer):
        def copy(peer, slot):
            return pltpu.make_async_remote_copy(
                src_ref=src_of(peer), dst_ref=recv.at[slot],
                send_sem=ss.at[e, peer], recv_sem=rs.at[e, slot],
                device_id={axis: target(peer)}, device_id_type=MESH,
            )

        def start():
            def body(off):
                copy(lax.rem(me + off, n), me).start()
            loop(1, n, body)

        def wait():
            def body(off):
                peer = lax.rem(me + off, n)
                copy(peer, peer).wait_recv()
                copy(peer, me).wait_send()
            loop(1, n, body)

        return start, wait

    def to_core(src, recv, e):
        return pltpu.make_async_remote_copy(
            src_ref=src, dst_ref=recv, send_sem=c_ss.at[e], recv_sem=c_rs.at[e],
            device_id={"dp": dp + 1 - 2 * core}, device_id_type=MESH,
        )

    def to_chips(src_of, recv, e):
        return spread(
            src_of, recv, a_ss, a_rs, e, "dp", chip, nchip, lambda peer: 2 * peer + core
        )

    a_i = lax.broadcasted_iota(jnp.int32, (width, width), 0)
    b_i = lax.broadcasted_iota(jnp.int32, (width, width), 1)
    perm[...] = jnp.where((a_i % S) * t_count + a_i // S == b_i, 1.0, 0.0).astype(BF16)
    permt[...] = jnp.where((b_i % S) * t_count + b_i // S == a_i, 1.0, 0.0).astype(BF16)
    j_i = lax.broadcasted_iota(jnp.int32, (width, C), 0)
    col[...] = (j_i % S) * t_count + j_i // S

    def ends(body):
        body(0)
        body(npair - 1)

    def input_rows(r0, pair):
        x = dot(perm[...], jnp.concatenate(pair, axis=1))
        kept = []
        for k in range(2):
            v = x[:, k * C:(k + 1) * C]
            a = jnp.where(inside(r0 + k), v * sigmoid(v), 0.0).astype(BF16)
            put(act, r0 + k + 2, a)
            kept.append(v.astype(BF16))
        return kept

    def stage_input(i):
        kept = input_rows(2 * i, [lat[2 * i], lat[2 * i + 1]])
        for k in range(2):
            latp[2 * i + k] = kept[k]

    many = npair // 2

    def stage_inputs(g):
        for k in range(many):
            latents_in(many * g + k).wait()
        for k in range(many):
            stage_input(many * g + k)

    loop(0, 2, stage_inputs)
    pl.semaphore_wait(barrier, ndp + nslab - 2)
    exchange_start(latent_halo)

    for copy in loads:
        copy.wait()
    scale = bs_ref[bk_ref[0]]
    row3 = lax.broadcasted_iota(jnp.int32, (3, rows, width), 1) + slab * rows
    lane3 = lax.broadcasted_iota(jnp.int32, (3, rows, width), 2)
    graded = jnp.where((row3 < height) & (lane3 < limit), img_ref[...].astype(F32) * scale, 0.0)
    graded = graded.reshape(3 * rows, width)
    lane = lax.broadcasted_iota(jnp.int32, (3 * rows, width), 1)
    shifted = [
        jnp.where(lane == width - 1, 0.0, pltpu.roll(graded, width - 1, 1)),
        graded,
        jnp.where(lane == 0, 0.0, pltpu.roll(graded, 1, 1)),
    ]
    stacked = jnp.concatenate([s.astype(BF16) for s in shifted], axis=0)
    gstage[...] = jnp.zeros_like(gstage)
    placed = dot(stacked, permt[...])
    for k in range(width // C):
        gstage[k, 0:9 * rows] = placed[:, k * C:(k + 1) * C]
        for r in range(rows):
            gimg[r + 1, :, k * C:(k + 1) * C] = gstage[k, pl.ds(r, 16, stride=rows), :].astype(BF16)

    halo_start(gimg, 1)

    zero = jnp.zeros((C, C), BF16)

    def weights(c, ref, flip):
        def tap(p, q):
            n = 3 * p + q
            return ref[(8 - n) * C:(9 - n) * C, :].T if flip else ref[n * C:(n + 1) * C, :]

        for j in range(1, 3):
            for q in range(3):
                at = (3 * (j - 1) + q) * C
                for k in range(2):
                    wi[c, at:at + C, k * C:(k + 1) * C] = tap(j - k, q)
        for k in range(2):
            wo[c, k, 0:C, 0:C] = tap(2 * k, 0)
            wo[c, k, 0:C, C:] = zero
            wo[c, k, C:, 0:C] = tap(2 * k, 1)
            wo[c, k, C:, C:] = tap(2 * k, 2)

    weights(0, w1_ref, False)
    weights(1, w2_ref, False)
    ci4f[...] = jnp.zeros_like(ci4f)
    for p in range(3):
        for q in range(3):
            piece = ci_ref[:, (3 * p + q) * C:(3 * p + q + 1) * C].astype(F32)
            for k in range(2):
                at = (2 - p + k) * 16 + q * 3
                ci4f[at:at + 3, k * C:(k + 1) * C] = piece
    ci4[...] = ci4f[...].astype(BF16)

    def conv(src, c, i):
        taps = [
            src[2 * i + j, q:q + t_count].reshape(width, C) for j in (1, 2) for q in range(3)
        ]
        inner = dot(jnp.concatenate(taps, axis=1), wi[c])
        done = []
        for k in range(2):
            pair = [
                src[2 * i + 3 * k, q:q + t_count + 1].reshape(width + S, C) for q in range(2)
            ]
            outer = dot(jnp.concatenate(pair, axis=1), wo[c, k])
            done.append(inner[:, k * C:(k + 1) * C] + outer[0:width, 0:C] + outer[S:, C:])
        return done

    def stage_one(i):
        y = conv(act, 0, i)
        for k in range(2):
            hb = y[k].astype(BF16)
            h1[2 * i + k] = hb
            hf = hb.astype(F32)
            m = jnp.where(inside(2 * i - 1 + k), hf * sigmoid(hf), 0.0).astype(BF16)
            put(mid, 2 * i + k, m)

    loop(1, npair, stage_one, npair - 1)

    sums[...] = jnp.zeros_like(sums)

    def fold(v):
        return jnp.sum(v.reshape(width // 8, 8, C), axis=0)

    def stage_two(i):
        y = conv(mid, 1, i)
        for k in range(2):
            r = 2 * i + k
            v = y[k] + latp[r].astype(F32)
            h2[r] = v
            masked = jnp.where(inside(r), v, 0.0)
            sums[0] += fold(masked)
            sums[1] += fold(masked * v)

    loop(1, npair - 1, stage_two, 3)

    exchange_wait(latent_halo)

    @pl.when(slab == 0)
    def _():
        lath[0] = jnp.zeros(lath.shape[1:], lath.dtype)

    @pl.when(slab == nslab - 1)
    def _():
        lath[1] = jnp.zeros(lath.shape[1:], lath.dtype)

    input_rows(-2, [lath[0, 0], lath[0, 1]])
    input_rows(rows, [lath[1, 0], lath[1, 1]])
    stage_one(0)
    stage_one(npair)
    ends(stage_two)

    def stats(e):
        stat_send[e, 0:1] = jnp.sum(sums[2 * e], axis=0, keepdims=True)
        stat_send[e, 1:2] = jnp.sum(sums[2 * e + 1], axis=0, keepdims=True)
        stat_recv[e, slab] = stat_send[e]
        return spread(
            lambda peer: stat_send.at[e], stat_recv.at[e], stat_ss, stat_rs, e, "slab", slab, nslab
        )

    def stat_total(e):
        total = stat_recv[e, 0]
        for k in range(1, nslab):
            total = total + stat_recv[e, k]
        return total

    for e in range(2):
        stat_send[e] = jnp.zeros(stat_send.shape[1:], F32)
    start, wait = stats(0)
    start()

    halo_wait(gimg, 1)

    def stage_image(i):
        y = lax.dot_general(
            gimg[pl.ds(2 * i, 4)].reshape(64, width), ci4[...], (((0,), (0,)), ((), ())),
            preferred_element_type=F32,
        )
        for k in range(2):
            gs[2 * i + k] = jnp.where(inside(2 * i + k), y[:, k * C:(k + 1) * C], 0.0)

    loop(0, npair, stage_image, 4)
    weights(2, w2_ref, True)
    weights(3, w1_ref, True)

    def slopes(kept, off, out):
        def body(r):
            v = kept[r + off].astype(F32)
            t = sigmoid(v)
            out[r] = jnp.where(inside(r), t + v * t * (1.0 - t), 0.0)
        loop(0, rows, body)

    slopes(h1, 1, slope1)
    wait()

    total = stat_total(0)
    mean = group_total(total[0:1]) / count
    rstd = lax.rsqrt(group_total(total[1:2]) / count - mean * mean + NORM_EPS)
    gain = gain_ref[...]
    bias = bias_ref[...]

    c1 = rstd * gain

    def stage_norm(r):
        centred = h2[r] - mean
        v = centred * c1 + bias
        s = sigmoid(v)
        vs = v * s
        nact[r] = jnp.where(inside(r), vs, 0.0).astype(BF16)
        g = gs[r] * (s + vs * (1.0 - s))
        gs[r] = g
        sums[2] += fold(g)
        sums[3] += fold(g * centred)

    loop(0, rows, stage_norm)
    start, wait = stats(1)
    start()

    imgacc[...] = jnp.zeros_like(imgacc)

    def stage_imgw(i):
        imgacc[...] += dot(
            gimg[pl.ds(2 * i, 4)].reshape(64, width),
            jnp.concatenate([nact[2 * i], nact[2 * i + 1]], axis=1),
        )

    loop(0, npair, stage_imgw, 4)
    flat[0:48] = imgacc[0:48, 0:C] + imgacc[16:64, C:2 * C]
    flat[9:10] = jnp.sum(sums[3], axis=0, keepdims=True) * rstd
    flat[10:11] = jnp.sum(sums[2], axis=0, keepdims=True)
    small_c[...] = flat[0:48].astype(BF16)
    to_core(small_c, small_rc, 0).start()

    def transposed(src, off, dst):
        def body(row):
            dst[row] = src[row + off, 1:t_count + 1].reshape(width, C).T
        loop(0, last + 1, body, 3)

    slopes(latp, 0, slope0)
    transposed(mid, 0, midt)
    transposed(act, 1, actt)
    wait()

    total = stat_total(1)
    c0 = rstd * (group_total(total[0:1] * gain) / count)
    c2 = rstd * rstd * (rstd * group_total(total[1:2] * gain) / count)

    def stage_grad_two(r):
        g = jnp.where(inside(r), gs[r] * c1 - c0 - (h2[r] - mean) * c2, 0.0).astype(BF16)
        put(b2, r + 1, g)

    stage_grad_two(0)
    stage_grad_two(rows - 1)
    halo_start(b2, 3)
    loop(1, rows - 1, stage_grad_two, 2)

    def weight_grad(at, b):
        acc[...] = jnp.zeros_like(acc)

        def piece(row, q):
            return b[row, 2 - q:2 - q + t_count].reshape(width, C)

        many = min(4, npair)

        def body(i):
            firsts = [2 * (i * many + u) for u in range(many)]
            lhs = jnp.concatenate(
                [at[pl.ds(r + k, 3)].reshape(3 * C, width) for r in firsts for k in range(2)], axis=1
            )
            rhs = jnp.concatenate(
                [
                    jnp.concatenate([piece(r + 1 + k, q) for q in range(2)], axis=1)
                    for r in firsts for k in range(2)
                ],
                axis=0,
            )
            acc[:, 0:2 * C] += dot(lhs, rhs)
            lhs = jnp.concatenate(
                [at[pl.ds(r, 4)].reshape(4 * C, width) for r in firsts], axis=1
            )
            rhs = jnp.concatenate(
                [jnp.concatenate([piece(r + 1 + k, 2) for k in range(2)], axis=1) for r in firsts],
                axis=0,
            )
            z = dot(lhs, rhs)
            acc[:, 2 * C:] += z[0:3 * C, 0:C] + z[C:, C:]

        loop(0, npair // many, body)

    def scatter(e):
        for p in range(3):
            for q in range(3):
                flat[(3 * p + q) * C:(3 * p + q + 1) * C] = acc[p * C:(p + 1) * C, q * C:(q + 1) * C]

        def body(d):
            send_c[e, lax.rem(d, 2), d // 2, 0:blk] = flat[
                pl.ds(pl.multiple_of(d * blk, 8), blk)
            ].astype(BF16)
        loop(0, ndp, body)
        copy = to_core(send_c.at[e, 1 - core], recv_c.at[e], 1 + e)
        copy.start()
        return copy

    def chips(e):
        def body(k):
            both = send_c[e, core, k].astype(F32) + recv_c[e, k].astype(F32)
            send_a[e, k] = both.astype(BF16)
        loop(0, nchip, body)
        recv_a[e, chip] = send_a[e, chip]
        start, wait = to_chips(lambda peer: send_a.at[e, peer], recv_a.at[e], 1 + e)
        start()
        return wait

    def gather(e):
        part = recv_a[e, 0].astype(F32)
        for k in range(1, nchip):
            part = part + recv_a[e, k].astype(F32)
        send_b[e] = part.astype(BF16)
        recv_b[e, slab] = send_b[e]
        start, wait = spread(
            lambda peer: send_b.at[e], recv_b.at[e], b_ss, b_rs, 1 + e, "slab", slab, nslab
        )
        start()
        return wait

    def finish(e):
        part = recv_b[e, 0].astype(F32)
        for k in range(1, nslab):
            part = part + recv_b[e, k].astype(F32)
        gw_ref[1 - e] = part[0:blk] * pixel_scale

    send_c[...] = jnp.zeros_like(send_c)
    weight_grad(midt, b2)
    second = scatter(0)

    def stage_grad_one(i):
        y = conv(b2, 2, i)
        for k in range(2):
            r = 2 * i + k
            put(b1, r + 1, (y[k] * slope1[r]).astype(BF16))

    middle = 1 + (npair - 2) // 2
    loop(1, middle, stage_grad_one, 3)
    second.wait()
    second_wait = chips(0)
    to_core(small_c, small_rc, 0).wait()
    small_a[...] = (small_c[...].astype(F32) + small_rc[...].astype(F32)).astype(BF16)
    small_ra[chip] = small_a[...]
    small_start, small_wait = to_chips(lambda peer: small_a, small_ra, 0)
    small_start()
    loop(middle, npair - 1, stage_grad_one, 3)
    halo_wait(b2, 3)
    ends(stage_grad_one)
    halo_start(b1, 4)

    weight_grad(actt, b1)
    first = scatter(1)

    def stage_latents(i):
        y = conv(b1, 3, i)
        done = []
        for k in range(2):
            r = 2 * i + k
            g = y[k] * slope0[r]
            own = b2[r + 1, 1:t_count + 1].reshape(width, C).astype(F32)
            done.append((own + g).astype(BF16))
        z = dot(permt[...], jnp.concatenate(done, axis=1)).astype(BF16)
        for k in range(2):
            glp[2 * i + k] = z[:, k * C:(k + 1) * C]

    def latents_group(lo, hi):
        loop(lo, hi, stage_latents, hi - lo)
        for i in range(lo, hi):
            latents_out(i).start()

    latents_group(1, 2)
    first.wait()
    first_wait = chips(1)
    small_wait()
    part = small_ra[0].astype(F32)
    for k in range(1, nchip):
        part = part + small_ra[k].astype(F32)
    small_b[...] = part.astype(BF16)
    small_rb[slab] = small_b[...]
    small_b_start, small_b_wait = spread(
        lambda peer: small_b, small_rb, b_ss, b_rs, 0, "slab", slab, nslab
    )
    small_b_start()
    second_wait()
    second_b_wait = gather(0)
    latents_group(2, npair - 1)
    first_wait()
    first_b_wait = gather(1)
    halo_wait(b1, 4)
    ends(stage_latents)
    ends(lambda i: latents_out(i).start())

    small_b_wait()
    part = small_rb[0].astype(F32)
    for k in range(1, nslab):
        part = part + small_rb[k].astype(F32)
    part = part * pixel_scale
    gn_ref[0] = part[9:10]
    gn_ref[1] = part[10:11]
    for p in range(3):
        for q in range(3):
            at = (2 - p) * 16 + q * 3
            gci_ref[:, (3 * p + q) * C:(3 * p + q + 1) * C] = part[at:at + 3]
    second_b_wait()
    finish(0)
    first_b_wait()
    finish(1)
    loop(0, npair, lambda i: latents_out(i).wait())


def unload(parts, gl_in, gw_in, gci_in, gn_in, gw1, gw2, gci, gg, gb, gl, gl_buf, gw_buf, gci_buf, gn_buf, sem):
    step = gl_buf.shape[0] // parts
    moves = [(gw_in.at[0], gw_buf.at[0], gw1), (gw_in.at[1], gw_buf.at[1], gw2), (gci_in, gci_buf, gci)]
    moves += [(gn_in.at[0], gn_buf.at[0], gg), (gn_in.at[1], gn_buf.at[1], gb)]
    for i in range(parts):
        rows = pl.ds(i * step, step)
        moves.append((gl_in.at[rows], gl_buf.at[rows], gl.at[rows]))
    into = [pltpu.make_async_copy(m[0], m[1], sem.at[0, i]) for i, m in enumerate(moves)]
    back = [pltpu.make_async_copy(m[1], m[2], sem.at[1, i]) for i, m in enumerate(moves)]
    order = list(range(5, 5 + parts)) + list(range(5))
    for i in order:
        into[i].start()
    for i in order:
        into[i].wait()
        back[i].start()
    for i in order:
        back[i].wait()


def shards(
    latents, image_grad, heights, widths, buckets, bucket_scale,
    conv_first, conv_second, conv_image, norm_gain, norm_bias,
):
    images, rows, width, channels = latents.shape
    ndp = lax.axis_size("dp")
    nslab = lax.axis_size("slab")
    t_count = width // S
    pixel_scale = 1.0 / math.sqrt(images * ndp * rows * nslab * width)
    blk = 9 * C // ndp
    pad = -(-blk // 16) * 16
    vmem = pl.BlockSpec(memory_space=pltpu.VMEM)
    smem = pl.BlockSpec(memory_space=pltpu.SMEM)
    nchip = ndp // 2
    edge = (rows + 2, t_count + 2, S, C)
    wide = (rows + 4, t_count + 2, S, C)
    scratch = [
        pltpu.VMEM(image_grad.shape[1:], BF16),
        pltpu.VMEM(conv_first.shape, BF16),
        pltpu.VMEM(conv_second.shape, BF16),
        pltpu.SemaphoreType.DMA((3,)),
        pltpu.VMEM((rows, width, C), BF16),
        pltpu.VMEM((2, 2, width, C), BF16),
        pltpu.VMEM((rows, width, C), BF16),
        pltpu.VMEM((rows, width, C), F32),
        pltpu.VMEM((rows, width, C), F32),
        pltpu.VMEM((width, width), BF16),
        pltpu.VMEM((width, width), BF16),
        pltpu.VMEM((width, C), jnp.int32),
        pltpu.VMEM((rows, width, C), BF16),
        pltpu.VMEM(wide, BF16),
        pltpu.VMEM(edge, BF16),
        pltpu.VMEM((rows + 2, C, width), BF16),
        pltpu.VMEM((rows + 2, C, width), BF16),
        pltpu.VMEM((rows + 2, width, C), BF16),
        pltpu.VMEM((rows, width, C), F32),
        pltpu.VMEM((rows, width, C), F32),
        pltpu.VMEM((rows, width, C), BF16),
        pltpu.VMEM(edge, BF16),
        pltpu.VMEM(edge, BF16),
        pltpu.VMEM((4, 6 * C, 2 * C), BF16),
        pltpu.VMEM((4, 2, 2 * C, 2 * C), BF16),
        pltpu.VMEM((64, 2 * C), F32),
        pltpu.VMEM((64, 2 * C), BF16),
        pltpu.VMEM((width // C, 16 * rows, C), F32),
        pltpu.VMEM((rows + 2, 16, width), BF16),
        pltpu.VMEM((3 * C, 3 * C), F32),
        pltpu.VMEM((9 * C, C), F32),
        pltpu.VMEM((64, 2 * C), F32),
        pltpu.VMEM((4, 8, C), F32),
        pltpu.VMEM((2, 8, C), F32),
        pltpu.VMEM((2, nslab, 8, C), F32),
        pltpu.VMEM((2, 2, nchip, pad, C), BF16),
        pltpu.VMEM((2, nchip, pad, C), BF16),
        pltpu.VMEM((2, nchip, pad, C), BF16),
        pltpu.VMEM((2, nchip, pad, C), BF16),
        pltpu.VMEM((2, pad, C), BF16),
        pltpu.VMEM((2, nslab, pad, C), BF16),
        pltpu.VMEM((48, C), BF16),
        pltpu.VMEM((48, C), BF16),
        pltpu.VMEM((48, C), BF16),
        pltpu.VMEM((nchip, 48, C), BF16),
        pltpu.VMEM((48, C), BF16),
        pltpu.VMEM((nslab, 48, C), BF16),
        pltpu.SemaphoreType.DMA((2, rows // 2)),
        pltpu.SemaphoreType.DMA((5, 2)),
        pltpu.SemaphoreType.DMA((5, 2)),
        pltpu.SemaphoreType.DMA((2, nslab)),
        pltpu.SemaphoreType.DMA((2, nslab)),
        pltpu.SemaphoreType.DMA((3,)),
        pltpu.SemaphoreType.DMA((3,)),
        pltpu.SemaphoreType.DMA((3, nchip)),
        pltpu.SemaphoreType.DMA((3, nchip)),
        pltpu.SemaphoreType.DMA((3, nslab)),
        pltpu.SemaphoreType.DMA((3, nslab)),
    ]
    anywhere = pl.BlockSpec(memory_space=pl.ANY)
    staged = pl.pallas_call(
        functools.partial(kernel, ndp, nslab, rows, width, pixel_scale),
        out_shape=(
            jax.ShapeDtypeStruct((rows, width, C), BF16),
            jax.ShapeDtypeStruct((2, blk, C), F32),
            jax.ShapeDtypeStruct((3, 9 * C), F32),
            jax.ShapeDtypeStruct((2, 1, C), F32),
        ),
        in_specs=[anywhere, anywhere, smem, smem, smem, smem, anywhere, anywhere, vmem, vmem, vmem],
        out_specs=(anywhere, vmem, vmem, vmem),
        scratch_shapes=scratch,
        compiler_params=pltpu.CompilerParams(
            collective_id=0, has_side_effects=True, vmem_limit_bytes=60 * 2**20
        ),
        cost_estimate=pl.CostEstimate(
            flops=int(1.6e10), bytes_accessed=5 * 2**20, transcendentals=5 * 2**20
        ),
    )(
        latents[0], image_grad[0], heights, widths, buckets, bucket_scale,
        conv_first, conv_second, conv_image, norm_gain[None], norm_bias[None],
    )
    parts = 4
    gw1, gw2, gci, gg, gb, gl = pl.pallas_call(
        functools.partial(unload, parts),
        out_shape=(
            jax.ShapeDtypeStruct((blk, C), F32),
            jax.ShapeDtypeStruct((blk, C), F32),
            jax.ShapeDtypeStruct((3, 9 * C), F32),
            jax.ShapeDtypeStruct((1, C), F32),
            jax.ShapeDtypeStruct((1, C), F32),
            jax.ShapeDtypeStruct((rows, width, C), BF16),
        ),
        in_specs=[anywhere] * 4,
        out_specs=(anywhere,) * 6,
        scratch_shapes=[
            pltpu.VMEM((rows, width, C), BF16),
            pltpu.VMEM((2, blk, C), F32),
            pltpu.VMEM((3, 9 * C), F32),
            pltpu.VMEM((2, 1, C), F32),
            pltpu.SemaphoreType.DMA((2, parts + 5)),
        ],
        compiler_params=pltpu.CompilerParams(vmem_limit_bytes=60 * 2**20),
    )(*staged)
    return gw1, gw2, gci, gg[0], gb[0], gl[None]


def solution(mesh):
    placed = (
        P("dp", "slab", None, None),
        P("dp", None, "slab", None),
        P("dp"),
        P("dp"),
        P("dp"),
        P(),
        P(),
        P(),
        P(),
        P(),
        P(),
    )
    return jax.shard_map(
        shards,
        mesh=mesh,
        in_specs=placed,
        out_specs=(P("dp", None), P("dp", None), P(), P(), P(), P("dp", "slab", None, None)),
        check_vma=False,
    )
```

```python
import functools
import math

import jax
import jax.numpy as jnp
from jax import lax
from jax.experimental import pallas as pl
from jax.experimental.pallas import tpu as pltpu
from jax.sharding import PartitionSpec as P

MESH = pl.DeviceIdType.MESH
F32 = jnp.float32
BF16 = jnp.bfloat16
PER_GROUP = 4
NORM_EPS = 1e-06
S = 16
C = 128


def dot(a, b):
    return jnp.dot(a, b, preferred_element_type=F32)


def sigmoid(v):
    return 0.5 * jnp.tanh(0.5 * v) + 0.5


def group_total(v):
    lane = lax.broadcasted_iota(jnp.int32, v.shape, 1)
    v = v + jnp.where(lane % 2 == 0, pltpu.roll(v, C - 1, 1), pltpu.roll(v, 1, 1))
    return v + jnp.where(lane % 4 < 2, pltpu.roll(v, C - 2, 1), pltpu.roll(v, 2, 1))


def kernel(
    ndp, nslab, rows, width, pixel_scale,
    lat_ref, img_in, h_ref, w_ref, bk_ref, bs_ref, w1_in, w2_in, ci_ref, gain_ref, bias_ref,
    out_ref, gw_ref, gci_ref, gn_ref,
    img_ref, w1_ref, w2_ref, load_sem, lat, lath, glp, slope0, slope1, perm, permt, col, latp, act, mid, actt, midt, h1, h2, gs, nact, b2, b1,
    wi, wo, ci4f, ci4, gstage, gimg, acc, flat, imgacc, sums, stat_send, stat_recv,
    send_c, recv_c, send_a, recv_a, send_b, recv_b,
    small_c, small_rc, small_a, small_ra, small_b, small_rb,
    io_sem, halo_s, halo_r, stat_ss, stat_rs, c_ss, c_rs, a_ss, a_rs, b_ss, b_rs,
):
    t_count = width // S
    last = rows + 1
    npair = rows // 2
    blk = (9 * C) // ndp
    nchip = ndp // 2
    dp = lax.axis_index("dp")
    slab = lax.axis_index("slab")
    core = lax.rem(dp, 2)
    chip = dp // 2

    def latents_in(i):
        part = pl.ds(2 * i, 2)
        return pltpu.make_async_copy(lat_ref.at[part], lat.at[part], io_sem.at[0, i])

    def latents_out(i):
        part = pl.ds(2 * i, 2)
        return pltpu.make_async_copy(glp.at[part], out_ref.at[part], io_sem.at[1, i])

    lax.fori_loop(0, npair, lambda i, _: (latents_in(i).start(), 0)[1], 0)
    loads = [
        pltpu.make_async_copy(src, dst, load_sem.at[i])
        for i, (src, dst) in enumerate(((img_in, img_ref), (w1_in, w1_ref), (w2_in, w2_ref)))
    ]
    for copy in loads:
        copy.start()

    barrier = pltpu.get_barrier_semaphore()

    def greet(axis, me, n):
        def body(off, _):
            pl.semaphore_signal(
                barrier, inc=1, device_id={axis: lax.rem(me + off, n)}, device_id_type=MESH
            )
            return 0
        lax.fori_loop(1, n, body, 0)

    greet("slab", slab, nslab)
    greet("dp", dp, ndp)

    height = h_ref[0]
    limit = w_ref[0]
    count = (height * limit * PER_GROUP).astype(F32)

    def inside(r):
        at = slab * rows + r
        return col[...] < jnp.where((at >= 0) & (at < height), limit, 0)

    def loop(lo, hi, body, unroll=1):
        if hi - lo <= unroll:
            for i in range(lo, hi):
                body(i)
            return
        assert (hi - lo) % unroll == 0

        def step(i, _):
            for k in range(unroll):
                body(lo + i * unroll + k)
            return 0
        lax.fori_loop(0, (hi - lo) // unroll, step, 0)

    def put(ref, row, a):
        ref[row, 1:t_count + 1] = a.reshape(t_count, S, C)
        sub = lax.broadcasted_iota(jnp.int32, (S, C), 0)
        low = pltpu.roll(a[width - S:].astype(F32), 1, 0)
        ref[row, 0] = jnp.where(sub == 0, 0.0, low).astype(BF16)
        high = pltpu.roll(a[:S].astype(F32), S - 1, 0)
        ref[row, t_count + 1] = jnp.where(sub == S - 1, 0.0, high).astype(BF16)

    def neighbour(src, dst, e, d):
        to = lax.rem(slab + (1 if d else nslab - 1), nslab)
        return pltpu.make_async_remote_copy(
            src_ref=src, dst_ref=dst, send_sem=halo_s.at[e, d], recv_sem=halo_r.at[e, d],
            device_id={"slab": to}, device_id_type=MESH,
        )

    def halo(ref, e, d):
        src, dst = (last - 1, 0) if d else (1, last)
        return neighbour(ref.at[src], ref.at[dst], e, d)

    def latent_halo(d):
        src = lat_ref.at[pl.ds(rows - 2 if d else 0, 2)]
        return neighbour(src, lath.at[1 - d], 0, d)

    above, below = slab > 0, slab < nslab - 1

    def exchange_start(copy):
        @pl.when(above)
        def _():
            copy(0).start()

        @pl.when(below)
        def _():
            copy(1).start()

    def exchange_wait(copy):
        @pl.when(above)
        def _():
            copy(0).wait_send()
            copy(1).wait_recv()

        @pl.when(below)
        def _():
            copy(1).wait_send()
            copy(0).wait_recv()

    def halo_start(ref, e):
        exchange_start(lambda d: halo(ref, e, d))

    def halo_wait(ref, e):
        exchange_wait(lambda d: halo(ref, e, d))

        @pl.when(slab == 0)
        def _():
            ref[0] = jnp.zeros(ref.shape[1:], ref.dtype)

        @pl.when(slab == nslab - 1)
        def _():
            ref[last] = jnp.zeros(ref.shape[1:], ref.dtype)

    def spread(src_of, recv, ss, rs, e, axis, me, n, target=lambda peer: peer):
        def copy(peer, slot):
            return pltpu.make_async_remote_copy(
                src_ref=src_of(peer), dst_ref=recv.at[slot],
                send_sem=ss.at[e, peer], recv_sem=rs.at[e, slot],
                device_id={axis: target(peer)}, device_id_type=MESH,
            )

        def start():
            def body(off):
                copy(lax.rem(me + off, n), me).start()
            loop(1, n, body)

        def wait():
            def body(off):
                peer = lax.rem(me + off, n)
                copy(peer, peer).wait_recv()
                copy(peer, me).wait_send()
            loop(1, n, body)

        return start, wait

    def to_core(src, recv, e):
        return pltpu.make_async_remote_copy(
            src_ref=src, dst_ref=recv, send_sem=c_ss.at[e], recv_sem=c_rs.at[e],
            device_id={"dp": dp + 1 - 2 * core}, device_id_type=MESH,
        )

    def to_chips(src_of, recv, e):
        return spread(
            src_of, recv, a_ss, a_rs, e, "dp", chip, nchip, lambda peer: 2 * peer + core
        )

    a_i = lax.broadcasted_iota(jnp.int32, (width, width), 0)
    b_i = lax.broadcasted_iota(jnp.int32, (width, width), 1)
    perm[...] = jnp.where((a_i % S) * t_count + a_i // S == b_i, 1.0, 0.0).astype(BF16)
    permt[...] = jnp.where((b_i % S) * t_count + b_i // S == a_i, 1.0, 0.0).astype(BF16)
    j_i = lax.broadcasted_iota(jnp.int32, (width, C), 0)
    col[...] = (j_i % S) * t_count + j_i // S

    def ends(body):
        body(0)
        body(npair - 1)

    def input_rows(r0, pair):
        x = dot(perm[...], jnp.concatenate(pair, axis=1))
        kept = []
        for k in range(2):
            v = x[:, k * C:(k + 1) * C]
            a = jnp.where(inside(r0 + k), v * sigmoid(v), 0.0).astype(BF16)
            put(act, r0 + k + 2, a)
            kept.append(v.astype(BF16))
        return kept

    def stage_input(i):
        kept = input_rows(2 * i, [lat[2 * i], lat[2 * i + 1]])
        for k in range(2):
            latp[2 * i + k] = kept[k]

    many = npair // 2

    def stage_inputs(g):
        for k in range(many):
            latents_in(many * g + k).wait()
        for k in range(many):
            stage_input(many * g + k)

    stage_inputs(0)
    pl.semaphore_wait(barrier, ndp + nslab - 2)
    exchange_start(latent_halo)
    stage_inputs(1)

    for copy in loads:
        copy.wait()
    scale = bs_ref[bk_ref[0]]
    row3 = lax.broadcasted_iota(jnp.int32, (3, rows, width), 1) + slab * rows
    lane3 = lax.broadcasted_iota(jnp.int32, (3, rows, width), 2)
    graded = jnp.where((row3 < height) & (lane3 < limit), img_ref[...].astype(F32) * scale, 0.0)
    graded = graded.reshape(3 * rows, width)
    lane = lax.broadcasted_iota(jnp.int32, (3 * rows, width), 1)
    shifted = [
        jnp.where(lane == width - 1, 0.0, pltpu.roll(graded, width - 1, 1)),
        graded,
        jnp.where(lane == 0, 0.0, pltpu.roll(graded, 1, 1)),
    ]
    stacked = jnp.concatenate([s.astype(BF16) for s in shifted], axis=0)
    gstage[...] = jnp.zeros_like(gstage)
    placed = dot(stacked, permt[...])
    for k in range(width // C):
        gstage[k, 0:9 * rows] = placed[:, k * C:(k + 1) * C]
        for r in range(rows):
            gimg[r + 1, :, k * C:(k + 1) * C] = gstage[k, pl.ds(r, 16, stride=rows), :].astype(BF16)

    halo_start(gimg, 1)

    zero = jnp.zeros((C, C), BF16)

    def weights(c, ref, flip):
        def tap(p, q):
            n = 3 * p + q
            return ref[(8 - n) * C:(9 - n) * C, :].T if flip else ref[n * C:(n + 1) * C, :]

        for j in range(1, 3):
            for q in range(3):
                at = (3 * (j - 1) + q) * C
                for k in range(2):
                    wi[c, at:at + C, k * C:(k + 1) * C] = tap(j - k, q)
        for k in range(2):
            wo[c, k, 0:C, 0:C] = tap(2 * k, 0)
            wo[c, k, 0:C, C:] = zero
            wo[c, k, C:, 0:C] = tap(2 * k, 1)
            wo[c, k, C:, C:] = tap(2 * k, 2)

    weights(0, w1_ref, False)
    weights(1, w2_ref, False)
    ci4f[...] = jnp.zeros_like(ci4f)
    for p in range(3):
        for q in range(3):
            piece = ci_ref[:, (3 * p + q) * C:(3 * p + q + 1) * C].astype(F32)
            for k in range(2):
                at = (2 - p + k) * 16 + q * 3
                ci4f[at:at + 3, k * C:(k + 1) * C] = piece
    ci4[...] = ci4f[...].astype(BF16)

    def conv(src, c, i):
        taps = [
            src[2 * i + j, q:q + t_count].reshape(width, C) for j in (1, 2) for q in range(3)
        ]
        inner = dot(jnp.concatenate(taps, axis=1), wi[c])
        done = []
        for k in range(2):
            pair = [
                src[2 * i + 3 * k, q:q + t_count + 1].reshape(width + S, C) for q in range(2)
            ]
            outer = dot(jnp.concatenate(pair, axis=1), wo[c, k])
            done.append(inner[:, k * C:(k + 1) * C] + outer[0:width, 0:C] + outer[S:, C:])
        return done

    def stage_one(i):
        y = conv(act, 0, i)
        for k in range(2):
            hb = y[k].astype(BF16)
            h1[2 * i + k] = hb
            hf = hb.astype(F32)
            m = jnp.where(inside(2 * i - 1 + k), hf * sigmoid(hf), 0.0).astype(BF16)
            put(mid, 2 * i + k, m)

    loop(1, npair, stage_one, npair - 1)

    sums[...] = jnp.zeros_like(sums)

    def fold(v):
        return jnp.sum(v.reshape(width // 8, 8, C), axis=0)

    def stage_two(i):
        y = conv(mid, 1, i)
        for k in range(2):
            r = 2 * i + k
            v = y[k] + latp[r].astype(F32)
            h2[r] = v
            masked = jnp.where(inside(r), v, 0.0)
            sums[0] += fold(masked)
            sums[1] += fold(masked * v)

    loop(1, npair - 1, stage_two, 3)

    exchange_wait(latent_halo)

    @pl.when(slab == 0)
    def _():
        lath[0] = jnp.zeros(lath.shape[1:], lath.dtype)

    @pl.when(slab == nslab - 1)
    def _():
        lath[1] = jnp.zeros(lath.shape[1:], lath.dtype)

    input_rows(-2, [lath[0, 0], lath[0, 1]])
    input_rows(rows, [lath[1, 0], lath[1, 1]])
    stage_one(0)
    stage_one(npair)
    ends(stage_two)

    def stats(e):
        stat_send[e, 0:1] = jnp.sum(sums[2 * e], axis=0, keepdims=True)
        stat_send[e, 1:2] = jnp.sum(sums[2 * e + 1], axis=0, keepdims=True)
        stat_recv[e, slab] = stat_send[e]
        return spread(
            lambda peer: stat_send.at[e], stat_recv.at[e], stat_ss, stat_rs, e, "slab", slab, nslab
        )

    def stat_total(e):
        total = stat_recv[e, 0]
        for k in range(1, nslab):
            total = total + stat_recv[e, k]
        return total

    for e in range(2):
        stat_send[e] = jnp.zeros(stat_send.shape[1:], F32)
    start, wait = stats(0)
    start()

    halo_wait(gimg, 1)

    def stage_image(i):
        y = lax.dot_general(
            gimg[pl.ds(2 * i, 4)].reshape(64, width), ci4[...], (((0,), (0,)), ((), ())),
            preferred_element_type=F32,
        )
        for k in range(2):
            gs[2 * i + k] = jnp.where(inside(2 * i + k), y[:, k * C:(k + 1) * C], 0.0)

    loop(0, npair, stage_image, 4)
    weights(2, w2_ref, True)
    weights(3, w1_ref, True)

    def slopes(kept, off, out):
        def body(r):
            v = kept[r + off].astype(F32)
            t = sigmoid(v)
            out[r] = jnp.where(inside(r), t + v * t * (1.0 - t), 0.0)
        loop(0, rows, body)

    slopes(h1, 1, slope1)
    wait()

    total = stat_total(0)
    mean = group_total(total[0:1]) / count
    rstd = lax.rsqrt(group_total(total[1:2]) / count - mean * mean + NORM_EPS)
    gain = gain_ref[...]
    bias = bias_ref[...]

    c1 = rstd * gain

    def stage_norm(r):
        centred = h2[r] - mean
        v = centred * c1 + bias
        s = sigmoid(v)
        vs = v * s
        nact[r] = jnp.where(inside(r), vs, 0.0).astype(BF16)
        g = gs[r] * (s + vs * (1.0 - s))
        gs[r] = g
        sums[2] += fold(g)
        sums[3] += fold(g * centred)

    loop(0, rows, stage_norm)
    start, wait = stats(1)
    start()

    imgacc[...] = jnp.zeros_like(imgacc)

    def stage_imgw(i):
        imgacc[...] += dot(
            gimg[pl.ds(2 * i, 4)].reshape(64, width),
            jnp.concatenate([nact[2 * i], nact[2 * i + 1]], axis=1),
        )

    loop(0, npair, stage_imgw, 4)
    flat[0:48] = imgacc[0:48, 0:C] + imgacc[16:64, C:2 * C]
    flat[9:10] = jnp.sum(sums[3], axis=0, keepdims=True) * rstd
    flat[10:11] = jnp.sum(sums[2], axis=0, keepdims=True)
    small_c[...] = flat[0:48].astype(BF16)
    to_core(small_c, small_rc, 0).start()

    def transposed(src, off, dst):
        def body(row):
            dst[row] = src[row + off, 1:t_count + 1].reshape(width, C).T
        loop(0, last + 1, body, 3)

    slopes(latp, 0, slope0)
    transposed(mid, 0, midt)
    transposed(act, 1, actt)
    wait()

    total = stat_total(1)
    c0 = rstd * (group_total(total[0:1] * gain) / count)
    c2 = rstd * rstd * (rstd * group_total(total[1:2] * gain) / count)

    def stage_grad_two(r):
        g = jnp.where(inside(r), gs[r] * c1 - c0 - (h2[r] - mean) * c2, 0.0).astype(BF16)
        put(b2, r + 1, g)

    stage_grad_two(0)
    stage_grad_two(rows - 1)
    halo_start(b2, 3)
    loop(1, rows - 1, stage_grad_two, 2)

    def weight_grad(at, b):
        acc[...] = jnp.zeros_like(acc)

        def piece(row, q):
            return b[row, 2 - q:2 - q + t_count].reshape(width, C)

        many = min(4, npair)

        def body(i):
            firsts = [2 * (i * many + u) for u in range(many)]
            lhs = jnp.concatenate(
                [at[pl.ds(r + k, 3)].reshape(3 * C, width) for r in firsts for k in range(2)], axis=1
            )
            rhs = jnp.concatenate(
                [
                    jnp.concatenate([piece(r + 1 + k, q) for q in range(2)], axis=1)
                    for r in firsts for k in range(2)
                ],
                axis=0,
            )
            acc[:, 0:2 * C] += dot(lhs, rhs)
            lhs = jnp.concatenate(
                [at[pl.ds(r, 4)].reshape(4 * C, width) for r in firsts], axis=1
            )
            rhs = jnp.concatenate(
                [jnp.concatenate([piece(r + 1 + k, 2) for k in range(2)], axis=1) for r in firsts],
                axis=0,
            )
            z = dot(lhs, rhs)
            acc[:, 2 * C:] += z[0:3 * C, 0:C] + z[C:, C:]

        loop(0, npair // many, body)

    def scatter(e):
        for p in range(3):
            for q in range(3):
                flat[(3 * p + q) * C:(3 * p + q + 1) * C] = acc[p * C:(p + 1) * C, q * C:(q + 1) * C]

        def body(d):
            send_c[e, lax.rem(d, 2), d // 2, 0:blk] = flat[
                pl.ds(pl.multiple_of(d * blk, 8), blk)
            ].astype(BF16)
        loop(0, ndp, body)
        copy = to_core(send_c.at[e, 1 - core], recv_c.at[e], 1 + e)
        copy.start()
        return copy

    def chips(e):
        def body(k):
            both = send_c[e, core, k].astype(F32) + recv_c[e, k].astype(F32)
            send_a[e, k] = both.astype(BF16)
        loop(0, nchip, body)
        recv_a[e, chip] = send_a[e, chip]
        start, wait = to_chips(lambda peer: send_a.at[e, peer], recv_a.at[e], 1 + e)
        start()
        return wait

    def gather(e):
        part = recv_a[e, 0].astype(F32)
        for k in range(1, nchip):
            part = part + recv_a[e, k].astype(F32)
        send_b[e] = part.astype(BF16)
        recv_b[e, slab] = send_b[e]
        start, wait = spread(
            lambda peer: send_b.at[e], recv_b.at[e], b_ss, b_rs, 1 + e, "slab", slab, nslab
        )
        start()
        return wait

    def finish(e):
        part = recv_b[e, 0].astype(F32)
        for k in range(1, nslab):
            part = part + recv_b[e, k].astype(F32)
        gw_ref[1 - e] = part[0:blk] * pixel_scale

    send_c[...] = jnp.zeros_like(send_c)
    weight_grad(midt, b2)
    second = scatter(0)

    def stage_grad_one(i):
        y = conv(b2, 2, i)
        for k in range(2):
            r = 2 * i + k
            put(b1, r + 1, (y[k] * slope1[r]).astype(BF16))

    middle = 1 + (npair - 2) // 2
    loop(1, middle, stage_grad_one, 3)
    second.wait()
    second_wait = chips(0)
    to_core(small_c, small_rc, 0).wait()
    small_a[...] = (small_c[...].astype(F32) + small_rc[...].astype(F32)).astype(BF16)
    small_ra[chip] = small_a[...]
    small_start, small_wait = to_chips(lambda peer: small_a, small_ra, 0)
    small_start()
    loop(middle, npair - 1, stage_grad_one, 3)
    halo_wait(b2, 3)
    ends(stage_grad_one)
    halo_start(b1, 4)

    weight_grad(actt, b1)
    first = scatter(1)

    def stage_latents(i):
        y = conv(b1, 3, i)
        done = []
        for k in range(2):
            r = 2 * i + k
            g = y[k] * slope0[r]
            own = b2[r + 1, 1:t_count + 1].reshape(width, C).astype(F32)
            done.append((own + g).astype(BF16))
        z = dot(permt[...], jnp.concatenate(done, axis=1)).astype(BF16)
        for k in range(2):
            glp[2 * i + k] = z[:, k * C:(k + 1) * C]

    def latents_group(lo, hi):
        loop(lo, hi, stage_latents, hi - lo)
        for i in range(lo, hi):
            latents_out(i).start()

    latents_group(1, 2)
    first.wait()
    first_wait = chips(1)
    small_wait()
    part = small_ra[0].astype(F32)
    for k in range(1, nchip):
        part = part + small_ra[k].astype(F32)
    small_b[...] = part.astype(BF16)
    small_rb[slab] = small_b[...]
    small_b_start, small_b_wait = spread(
        lambda peer: small_b, small_rb, b_ss, b_rs, 0, "slab", slab, nslab
    )
    small_b_start()
    second_wait()
    second_b_wait = gather(0)
    latents_group(2, npair - 1)
    first_wait()
    first_b_wait = gather(1)
    halo_wait(b1, 4)
    ends(stage_latents)
    ends(lambda i: latents_out(i).start())

    small_b_wait()
    part = small_rb[0].astype(F32)
    for k in range(1, nslab):
        part = part + small_rb[k].astype(F32)
    part = part * pixel_scale
    gn_ref[0] = part[9:10]
    gn_ref[1] = part[10:11]
    for p in range(3):
        for q in range(3):
            at = (2 - p) * 16 + q * 3
            gci_ref[:, (3 * p + q) * C:(3 * p + q + 1) * C] = part[at:at + 3]
    second_b_wait()
    finish(0)
    first_b_wait()
    finish(1)
    loop(0, npair, lambda i: latents_out(i).wait())


def unload(parts, gl_in, gw_in, gci_in, gn_in, gw1, gw2, gci, gg, gb, gl, gl_buf, gw_buf, gci_buf, gn_buf, sem):
    step = gl_buf.shape[0] // parts
    moves = [(gw_in.at[0], gw_buf.at[0], gw1), (gw_in.at[1], gw_buf.at[1], gw2), (gci_in, gci_buf, gci)]
    moves += [(gn_in.at[0], gn_buf.at[0], gg), (gn_in.at[1], gn_buf.at[1], gb)]
    for i in range(parts):
        rows = pl.ds(i * step, step)
        moves.append((gl_in.at[rows], gl_buf.at[rows], gl.at[rows]))
    into = [pltpu.make_async_copy(m[0], m[1], sem.at[0, i]) for i, m in enumerate(moves)]
    back = [pltpu.make_async_copy(m[1], m[2], sem.at[1, i]) for i, m in enumerate(moves)]
    order = list(range(5, 5 + parts)) + list(range(5))
    for i in order:
        into[i].start()
    for i in order:
        into[i].wait()
        back[i].start()
    for i in order:
        back[i].wait()


def shards(
    latents, image_grad, heights, widths, buckets, bucket_scale,
    conv_first, conv_second, conv_image, norm_gain, norm_bias,
):
    images, rows, width, channels = latents.shape
    ndp = lax.axis_size("dp")
    nslab = lax.axis_size("slab")
    t_count = width // S
    pixel_scale = 1.0 / math.sqrt(images * ndp * rows * nslab * width)
    blk = 9 * C // ndp
    pad = -(-blk // 16) * 16
    vmem = pl.BlockSpec(memory_space=pltpu.VMEM)
    smem = pl.BlockSpec(memory_space=pltpu.SMEM)
    nchip = ndp // 2
    edge = (rows + 2, t_count + 2, S, C)
    wide = (rows + 4, t_count + 2, S, C)
    scratch = [
        pltpu.VMEM(image_grad.shape[1:], BF16),
        pltpu.VMEM(conv_first.shape, BF16),
        pltpu.VMEM(conv_second.shape, BF16),
        pltpu.SemaphoreType.DMA((3,)),
        pltpu.VMEM((rows, width, C), BF16),
        pltpu.VMEM((2, 2, width, C), BF16),
        pltpu.VMEM((rows, width, C), BF16),
        pltpu.VMEM((rows, width, C), F32),
        pltpu.VMEM((rows, width, C), F32),
        pltpu.VMEM((width, width), BF16),
        pltpu.VMEM((width, width), BF16),
        pltpu.VMEM((width, C), jnp.int32),
        pltpu.VMEM((rows, width, C), BF16),
        pltpu.VMEM(wide, BF16),
        pltpu.VMEM(edge, BF16),
        pltpu.VMEM((rows + 2, C, width), BF16),
        pltpu.VMEM((rows + 2, C, width), BF16),
        pltpu.VMEM((rows + 2, width, C), BF16),
        pltpu.VMEM((rows, width, C), F32),
        pltpu.VMEM((rows, width, C), F32),
        pltpu.VMEM((rows, width, C), BF16),
        pltpu.VMEM(edge, BF16),
        pltpu.VMEM(edge, BF16),
        pltpu.VMEM((4, 6 * C, 2 * C), BF16),
        pltpu.VMEM((4, 2, 2 * C, 2 * C), BF16),
        pltpu.VMEM((64, 2 * C), F32),
        pltpu.VMEM((64, 2 * C), BF16),
        pltpu.VMEM((width // C, 16 * rows, C), F32),
        pltpu.VMEM((rows + 2, 16, width), BF16),
        pltpu.VMEM((3 * C, 3 * C), F32),
        pltpu.VMEM((9 * C, C), F32),
        pltpu.VMEM((64, 2 * C), F32),
        pltpu.VMEM((4, 8, C), F32),
        pltpu.VMEM((2, 8, C), F32),
        pltpu.VMEM((2, nslab, 8, C), F32),
        pltpu.VMEM((2, 2, nchip, pad, C), BF16),
        pltpu.VMEM((2, nchip, pad, C), BF16),
        pltpu.VMEM((2, nchip, pad, C), BF16),
        pltpu.VMEM((2, nchip, pad, C), BF16),
        pltpu.VMEM((2, pad, C), BF16),
        pltpu.VMEM((2, nslab, pad, C), BF16),
        pltpu.VMEM((48, C), BF16),
        pltpu.VMEM((48, C), BF16),
        pltpu.VMEM((48, C), BF16),
        pltpu.VMEM((nchip, 48, C), BF16),
        pltpu.VMEM((48, C), BF16),
        pltpu.VMEM((nslab, 48, C), BF16),
        pltpu.SemaphoreType.DMA((2, rows // 2)),
        pltpu.SemaphoreType.DMA((5, 2)),
        pltpu.SemaphoreType.DMA((5, 2)),
        pltpu.SemaphoreType.DMA((2, nslab)),
        pltpu.SemaphoreType.DMA((2, nslab)),
        pltpu.SemaphoreType.DMA((3,)),
        pltpu.SemaphoreType.DMA((3,)),
        pltpu.SemaphoreType.DMA((3, nchip)),
        pltpu.SemaphoreType.DMA((3, nchip)),
        pltpu.SemaphoreType.DMA((3, nslab)),
        pltpu.SemaphoreType.DMA((3, nslab)),
    ]
    anywhere = pl.BlockSpec(memory_space=pl.ANY)
    staged = pl.pallas_call(
        functools.partial(kernel, ndp, nslab, rows, width, pixel_scale),
        out_shape=(
            jax.ShapeDtypeStruct((rows, width, C), BF16),
            jax.ShapeDtypeStruct((2, blk, C), F32),
            jax.ShapeDtypeStruct((3, 9 * C), F32),
            jax.ShapeDtypeStruct((2, 1, C), F32),
        ),
        in_specs=[anywhere, anywhere, smem, smem, smem, smem, anywhere, anywhere, vmem, vmem, vmem],
        out_specs=(anywhere, vmem, vmem, vmem),
        scratch_shapes=scratch,
        compiler_params=pltpu.CompilerParams(
            collective_id=0, has_side_effects=True, vmem_limit_bytes=60 * 2**20
        ),
        cost_estimate=pl.CostEstimate(
            flops=int(1.6e10), bytes_accessed=5 * 2**20, transcendentals=5 * 2**20
        ),
    )(
        latents[0], image_grad[0], heights, widths, buckets, bucket_scale,
        conv_first, conv_second, conv_image, norm_gain[None], norm_bias[None],
    )
    parts = 4
    gw1, gw2, gci, gg, gb, gl = pl.pallas_call(
        functools.partial(unload, parts),
        out_shape=(
            jax.ShapeDtypeStruct((blk, C), F32),
            jax.ShapeDtypeStruct((blk, C), F32),
            jax.ShapeDtypeStruct((3, 9 * C), F32),
            jax.ShapeDtypeStruct((1, C), F32),
            jax.ShapeDtypeStruct((1, C), F32),
            jax.ShapeDtypeStruct((rows, width, C), BF16),
        ),
        in_specs=[anywhere] * 4,
        out_specs=(anywhere,) * 6,
        scratch_shapes=[
            pltpu.VMEM((rows, width, C), BF16),
            pltpu.VMEM((2, blk, C), F32),
            pltpu.VMEM((3, 9 * C), F32),
            pltpu.VMEM((2, 1, C), F32),
            pltpu.SemaphoreType.DMA((2, parts + 5)),
        ],
        compiler_params=pltpu.CompilerParams(vmem_limit_bytes=60 * 2**20),
    )(*staged)
    return gw1, gw2, gci, gg[0], gb[0], gl[None]


def solution(mesh):
    placed = (
        P("dp", "slab", None, None),
        P("dp", None, "slab", None),
        P("dp"),
        P("dp"),
        P("dp"),
        P(),
        P(),
        P(),
        P(),
        P(),
        P(),
    )
    return jax.shard_map(
        shards,
        mesh=mesh,
        in_specs=placed,
        out_specs=(P("dp", None), P("dp", None), P(), P(), P(), P("dp", "slab", None, None)),
        check_vma=False,
    )
```

```python
import functools
import math

import jax
import jax.numpy as jnp
from jax import lax
from jax.experimental import pallas as pl
from jax.experimental.pallas import tpu as pltpu
from jax.sharding import PartitionSpec as P

MESH = pl.DeviceIdType.MESH
F32 = jnp.float32
BF16 = jnp.bfloat16
PER_GROUP = 4
NORM_EPS = 1e-06
S = 16
C = 128


def dot(a, b):
    return jnp.dot(a, b, preferred_element_type=F32)


def sigmoid(v):
    return 0.5 * jnp.tanh(0.5 * v) + 0.5


def group_total(v):
    lane = lax.broadcasted_iota(jnp.int32, v.shape, 1)
    v = v + jnp.where(lane % 2 == 0, pltpu.roll(v, C - 1, 1), pltpu.roll(v, 1, 1))
    return v + jnp.where(lane % 4 < 2, pltpu.roll(v, C - 2, 1), pltpu.roll(v, 2, 1))


def kernel(
    ndp, nslab, rows, width, pixel_scale,
    lat_ref, img_in, h_ref, w_ref, bk_ref, bs_ref, w1_in, w2_in, ci_ref, gain_ref, bias_ref,
    out_ref, gw_ref, gci_ref, gn_ref,
    img_ref, w1_ref, w2_ref, load_sem, lat, lath, glp, slope0, slope1, perm, permt, col, latp, act, mid, actt, midt, h1, h2, gs, nact, b2, b1,
    wi, wo, ci4f, ci4, gstage, gimg, acc, flat, imgacc, sums, stat_send, stat_recv,
    send_c, recv_c, send_a, recv_a, send_b, recv_b,
    small_c, small_rc, small_a, small_ra, small_b, small_rb,
    io_sem, halo_s, halo_r, stat_ss, stat_rs, c_ss, c_rs, a_ss, a_rs, b_ss, b_rs,
):
    t_count = width // S
    last = rows + 1
    npair = rows // 2
    blk = (9 * C) // ndp
    nchip = ndp // 2
    dp = lax.axis_index("dp")
    slab = lax.axis_index("slab")
    core = lax.rem(dp, 2)
    chip = dp // 2

    def latents_in(i):
        part = pl.ds(2 * i, 2)
        return pltpu.make_async_copy(lat_ref.at[part], lat.at[part], io_sem.at[0, i])

    def latents_out(i):
        part = pl.ds(2 * i, 2)
        return pltpu.make_async_copy(glp.at[part], out_ref.at[part], io_sem.at[1, i])

    lax.fori_loop(0, npair, lambda i, _: (latents_in(i).start(), 0)[1], 0)
    loads = [
        pltpu.make_async_copy(src, dst, load_sem.at[i])
        for i, (src, dst) in enumerate(((img_in, img_ref), (w1_in, w1_ref), (w2_in, w2_ref)))
    ]
    for copy in loads:
        copy.start()

    barrier = pltpu.get_barrier_semaphore()

    def greet(axis, me, n):
        def body(off, _):
            pl.semaphore_signal(
                barrier, inc=1, device_id={axis: lax.rem(me + off, n)}, device_id_type=MESH
            )
            return 0
        lax.fori_loop(1, n, body, 0)

    greet("slab", slab, nslab)
    greet("dp", dp, ndp)

    height = h_ref[0]
    limit = w_ref[0]
    count = (height * limit * PER_GROUP).astype(F32)

    def inside(r):
        at = slab * rows + r
        return col[...] < jnp.where((at >= 0) & (at < height), limit, 0)

    def loop(lo, hi, body, unroll=1):
        if hi - lo <= unroll:
            for i in range(lo, hi):
                body(i)
            return
        assert (hi - lo) % unroll == 0

        def step(i, _):
            for k in range(unroll):
                body(lo + i * unroll + k)
            return 0
        lax.fori_loop(0, (hi - lo) // unroll, step, 0)

    def put(ref, row, a):
        ref[row, 1:t_count + 1] = a.reshape(t_count, S, C)
        sub = lax.broadcasted_iota(jnp.int32, (S, C), 0)
        low = pltpu.roll(a[width - S:].astype(F32), 1, 0)
        ref[row, 0] = jnp.where(sub == 0, 0.0, low).astype(BF16)
        high = pltpu.roll(a[:S].astype(F32), S - 1, 0)
        ref[row, t_count + 1] = jnp.where(sub == S - 1, 0.0, high).astype(BF16)

    def neighbour(src, dst, e, d):
        to = lax.rem(slab + (1 if d else nslab - 1), nslab)
        return pltpu.make_async_remote_copy(
            src_ref=src, dst_ref=dst, send_sem=halo_s.at[e, d], recv_sem=halo_r.at[e, d],
            device_id={"slab": to}, device_id_type=MESH,
        )

    def halo(ref, e, d):
        src, dst = (last - 1, 0) if d else (1, last)
        return neighbour(ref.at[src], ref.at[dst], e, d)

    def latent_halo(d):
        src = lat_ref.at[pl.ds(rows - 2 if d else 0, 2)]
        return neighbour(src, lath.at[1 - d], 0, d)

    above, below = slab > 0, slab < nslab - 1

    def exchange_start(copy):
        @pl.when(above)
        def _():
            copy(0).start()

        @pl.when(below)
        def _():
            copy(1).start()

    def exchange_wait(copy):
        @pl.when(above)
        def _():
            copy(0).wait_send()
            copy(1).wait_recv()

        @pl.when(below)
        def _():
            copy(1).wait_send()
            copy(0).wait_recv()

    def halo_start(ref, e):
        exchange_start(lambda d: halo(ref, e, d))

    def halo_wait(ref, e):
        exchange_wait(lambda d: halo(ref, e, d))

        @pl.when(slab == 0)
        def _():
            ref[0] = jnp.zeros(ref.shape[1:], ref.dtype)

        @pl.when(slab == nslab - 1)
        def _():
            ref[last] = jnp.zeros(ref.shape[1:], ref.dtype)

    def spread(src_of, recv, ss, rs, e, axis, me, n, target=lambda peer: peer):
        def copy(peer, slot):
            return pltpu.make_async_remote_copy(
                src_ref=src_of(peer), dst_ref=recv.at[slot],
                send_sem=ss.at[e, peer], recv_sem=rs.at[e, slot],
                device_id={axis: target(peer)}, device_id_type=MESH,
            )

        def start():
            def body(off):
                copy(lax.rem(me + off, n), me).start()
            loop(1, n, body)

        def wait():
            def body(off):
                peer = lax.rem(me + off, n)
                copy(peer, peer).wait_recv()
                copy(peer, me).wait_send()
            loop(1, n, body)

        return start, wait

    def to_core(src, recv, e):
        return pltpu.make_async_remote_copy(
            src_ref=src, dst_ref=recv, send_sem=c_ss.at[e], recv_sem=c_rs.at[e],
            device_id={"dp": dp + 1 - 2 * core}, device_id_type=MESH,
        )

    def to_chips(src_of, recv, e):
        return spread(
            src_of, recv, a_ss, a_rs, e, "dp", chip, nchip, lambda peer: 2 * peer + core
        )

    a_i = lax.broadcasted_iota(jnp.int32, (width, width), 0)
    b_i = lax.broadcasted_iota(jnp.int32, (width, width), 1)
    perm[...] = jnp.where((a_i % S) * t_count + a_i // S == b_i, 1.0, 0.0).astype(BF16)
    permt[...] = jnp.where((b_i % S) * t_count + b_i // S == a_i, 1.0, 0.0).astype(BF16)
    j_i = lax.broadcasted_iota(jnp.int32, (width, C), 0)
    col[...] = (j_i % S) * t_count + j_i // S

    def ends(body):
        body(0)
        body(npair - 1)

    def input_rows(r0, pair):
        x = dot(perm[...], jnp.concatenate(pair, axis=1))
        kept = []
        for k in range(2):
            v = x[:, k * C:(k + 1) * C]
            a = jnp.where(inside(r0 + k), v * sigmoid(v), 0.0).astype(BF16)
            put(act, r0 + k + 2, a)
            kept.append(v.astype(BF16))
        return kept

    def stage_input(i):
        kept = input_rows(2 * i, [lat[2 * i], lat[2 * i + 1]])
        for k in range(2):
            latp[2 * i + k] = kept[k]

    many = npair // 2

    def stage_inputs(g):
        for k in range(many):
            latents_in(many * g + k).wait()
        for k in range(many):
            stage_input(many * g + k)

    stage_inputs(0)
    pl.semaphore_wait(barrier, ndp + nslab - 2)
    exchange_start(latent_halo)
    stage_inputs(1)

    for copy in loads:
        copy.wait()
    scale = bs_ref[bk_ref[0]]
    row3 = lax.broadcasted_iota(jnp.int32, (3, rows, width), 1) + slab * rows
    lane3 = lax.broadcasted_iota(jnp.int32, (3, rows, width), 2)
    graded = jnp.where((row3 < height) & (lane3 < limit), img_ref[...].astype(F32) * scale, 0.0)
    graded = graded.reshape(3 * rows, width)
    lane = lax.broadcasted_iota(jnp.int32, (3 * rows, width), 1)
    shifted = [
        jnp.where(lane == width - 1, 0.0, pltpu.roll(graded, width - 1, 1)),
        graded,
        jnp.where(lane == 0, 0.0, pltpu.roll(graded, 1, 1)),
    ]
    stacked = jnp.concatenate([s.astype(BF16) for s in shifted], axis=0)
    gstage[...] = jnp.zeros_like(gstage)
    placed = dot(stacked, permt[...])
    for k in range(width // C):
        gstage[k, 0:9 * rows] = placed[:, k * C:(k + 1) * C]
        for r in range(rows):
            gimg[r + 1, :, k * C:(k + 1) * C] = gstage[k, pl.ds(r, 16, stride=rows), :].astype(BF16)

    halo_start(gimg, 1)

    zero = jnp.zeros((C, C), BF16)

    def weights(c, ref, flip):
        def tap(p, q):
            n = 3 * p + q
            return ref[(8 - n) * C:(9 - n) * C, :].T if flip else ref[n * C:(n + 1) * C, :]

        for j in range(1, 3):
            for q in range(3):
                at = (3 * (j - 1) + q) * C
                for k in range(2):
                    wi[c, at:at + C, k * C:(k + 1) * C] = tap(j - k, q)
        for k in range(2):
            wo[c, k, 0:C, 0:C] = tap(2 * k, 0)
            wo[c, k, 0:C, C:] = zero
            wo[c, k, C:, 0:C] = tap(2 * k, 1)
            wo[c, k, C:, C:] = tap(2 * k, 2)

    weights(0, w1_ref, False)
    weights(1, w2_ref, False)
    ci4f[...] = jnp.zeros_like(ci4f)
    for p in range(3):
        for q in range(3):
            piece = ci_ref[:, (3 * p + q) * C:(3 * p + q + 1) * C].astype(F32)
            for k in range(2):
                at = (2 - p + k) * 16 + q * 3
                ci4f[at:at + 3, k * C:(k + 1) * C] = piece
    ci4[...] = ci4f[...].astype(BF16)

    def conv(src, c, i):
        taps = [
            src[2 * i + j, q:q + t_count].reshape(width, C) for j in (1, 2) for q in range(3)
        ]
        inner = dot(jnp.concatenate(taps, axis=1), wi[c])
        done = []
        for k in range(2):
            pair = [
                src[2 * i + 3 * k, q:q + t_count + 1].reshape(width + S, C) for q in range(2)
            ]
            outer = dot(jnp.concatenate(pair, axis=1), wo[c, k])
            done.append(inner[:, k * C:(k + 1) * C] + outer[0:width, 0:C] + outer[S:, C:])
        return done

    def stage_one(i):
        y = conv(act, 0, i)
        for k in range(2):
            hb = y[k].astype(BF16)
            h1[2 * i + k] = hb
            hf = hb.astype(F32)
            m = jnp.where(inside(2 * i - 1 + k), hf * sigmoid(hf), 0.0).astype(BF16)
            put(mid, 2 * i + k, m)

    loop(1, npair, stage_one, npair - 1)

    sums[...] = jnp.zeros_like(sums)

    def fold(v):
        return jnp.sum(v.reshape(width // 8, 8, C), axis=0)

    def stage_two(i):
        y = conv(mid, 1, i)
        for k in range(2):
            r = 2 * i + k
            v = y[k] + latp[r].astype(F32)
            h2[r] = v
            masked = jnp.where(inside(r), v, 0.0)
            sums[0] += fold(masked)
            sums[1] += fold(masked * v)

    loop(1, npair - 1, stage_two, 3)

    def transposed(src, off, dst, lo, hi, unroll):
        def body(row):
            dst[row] = src[row + off, 1:t_count + 1].reshape(width, C).T
        loop(lo, hi, body, unroll)

    transposed(act, 1, actt, 1, last, 4)

    exchange_wait(latent_halo)

    @pl.when(slab == 0)
    def _():
        lath[0] = jnp.zeros(lath.shape[1:], lath.dtype)

    @pl.when(slab == nslab - 1)
    def _():
        lath[1] = jnp.zeros(lath.shape[1:], lath.dtype)

    input_rows(-2, [lath[0, 0], lath[0, 1]])
    input_rows(rows, [lath[1, 0], lath[1, 1]])
    stage_one(0)
    stage_one(npair)
    ends(stage_two)

    def stats(e):
        stat_send[e, 0:1] = jnp.sum(sums[2 * e], axis=0, keepdims=True)
        stat_send[e, 1:2] = jnp.sum(sums[2 * e + 1], axis=0, keepdims=True)
        stat_recv[e, slab] = stat_send[e]
        return spread(
            lambda peer: stat_send.at[e], stat_recv.at[e], stat_ss, stat_rs, e, "slab", slab, nslab
        )

    def stat_total(e):
        total = stat_recv[e, 0]
        for k in range(1, nslab):
            total = total + stat_recv[e, k]
        return total

    for e in range(2):
        stat_send[e] = jnp.zeros(stat_send.shape[1:], F32)
    start, wait = stats(0)
    start()

    halo_wait(gimg, 1)

    def stage_image(i):
        y = lax.dot_general(
            gimg[pl.ds(2 * i, 4)].reshape(64, width), ci4[...], (((0,), (0,)), ((), ())),
            preferred_element_type=F32,
        )
        for k in range(2):
            gs[2 * i + k] = jnp.where(inside(2 * i + k), y[:, k * C:(k + 1) * C], 0.0)

    loop(0, npair, stage_image, 4)
    weights(2, w2_ref, True)
    weights(3, w1_ref, True)

    def slopes(kept, off, out):
        def body(r):
            v = kept[r + off].astype(F32)
            t = sigmoid(v)
            out[r] = jnp.where(inside(r), t + v * t * (1.0 - t), 0.0)
        loop(0, rows, body)

    slopes(h1, 1, slope1)
    wait()

    total = stat_total(0)
    mean = group_total(total[0:1]) / count
    rstd = lax.rsqrt(group_total(total[1:2]) / count - mean * mean + NORM_EPS)
    gain = gain_ref[...]
    bias = bias_ref[...]

    c1 = rstd * gain

    def stage_norm(r):
        centred = h2[r] - mean
        v = centred * c1 + bias
        s = sigmoid(v)
        vs = v * s
        nact[r] = jnp.where(inside(r), vs, 0.0).astype(BF16)
        g = gs[r] * (s + vs * (1.0 - s))
        gs[r] = g
        sums[2] += fold(g)
        sums[3] += fold(g * centred)

    loop(0, rows, stage_norm)
    start, wait = stats(1)
    start()

    imgacc[...] = jnp.zeros_like(imgacc)

    def stage_imgw(i):
        imgacc[...] += dot(
            gimg[pl.ds(2 * i, 4)].reshape(64, width),
            jnp.concatenate([nact[2 * i], nact[2 * i + 1]], axis=1),
        )

    loop(0, npair, stage_imgw, 4)
    flat[0:48] = imgacc[0:48, 0:C] + imgacc[16:64, C:2 * C]
    flat[9:10] = jnp.sum(sums[3], axis=0, keepdims=True) * rstd
    flat[10:11] = jnp.sum(sums[2], axis=0, keepdims=True)
    small_c[...] = flat[0:48].astype(BF16)
    to_core(small_c, small_rc, 0).start()

    slopes(latp, 0, slope0)
    transposed(mid, 0, midt, 0, last + 1, 3)
    for row in (0, last):
        actt[row] = act[row + 1, 1:t_count + 1].reshape(width, C).T
    wait()

    total = stat_total(1)
    c0 = rstd * (group_total(total[0:1] * gain) / count)
    c2 = rstd * rstd * (rstd * group_total(total[1:2] * gain) / count)

    def stage_grad_two(r):
        g = jnp.where(inside(r), gs[r] * c1 - c0 - (h2[r] - mean) * c2, 0.0).astype(BF16)
        put(b2, r + 1, g)

    stage_grad_two(0)
    stage_grad_two(rows - 1)
    halo_start(b2, 3)
    loop(1, rows - 1, stage_grad_two, 2)

    def weight_grad(at, b):
        acc[...] = jnp.zeros_like(acc)

        def piece(row, q):
            return b[row, 2 - q:2 - q + t_count].reshape(width, C)

        many = min(4, npair)

        def body(i):
            firsts = [2 * (i * many + u) for u in range(many)]
            lhs = jnp.concatenate(
                [at[pl.ds(r + k, 3)].reshape(3 * C, width) for r in firsts for k in range(2)], axis=1
            )
            rhs = jnp.concatenate(
                [
                    jnp.concatenate([piece(r + 1 + k, q) for q in range(2)], axis=1)
                    for r in firsts for k in range(2)
                ],
                axis=0,
            )
            acc[:, 0:2 * C] += dot(lhs, rhs)
            lhs = jnp.concatenate(
                [at[pl.ds(r, 4)].reshape(4 * C, width) for r in firsts], axis=1
            )
            rhs = jnp.concatenate(
                [jnp.concatenate([piece(r + 1 + k, 2) for k in range(2)], axis=1) for r in firsts],
                axis=0,
            )
            z = dot(lhs, rhs)
            acc[:, 2 * C:] += z[0:3 * C, 0:C] + z[C:, C:]

        loop(0, npair // many, body)

    def scatter(e):
        for p in range(3):
            for q in range(3):
                flat[(3 * p + q) * C:(3 * p + q + 1) * C] = acc[p * C:(p + 1) * C, q * C:(q + 1) * C]

        def body(d):
            send_c[e, lax.rem(d, 2), d // 2, 0:blk] = flat[
                pl.ds(pl.multiple_of(d * blk, 8), blk)
            ].astype(BF16)
        loop(0, ndp, body)
        copy = to_core(send_c.at[e, 1 - core], recv_c.at[e], 1 + e)
        copy.start()
        return copy

    def chips(e):
        def body(k):
            both = send_c[e, core, k].astype(F32) + recv_c[e, k].astype(F32)
            send_a[e, k] = both.astype(BF16)
        loop(0, nchip, body)
        recv_a[e, chip] = send_a[e, chip]
        start, wait = to_chips(lambda peer: send_a.at[e, peer], recv_a.at[e], 1 + e)
        start()
        return wait

    def gather(e):
        part = recv_a[e, 0].astype(F32)
        for k in range(1, nchip):
            part = part + recv_a[e, k].astype(F32)
        send_b[e] = part.astype(BF16)
        recv_b[e, slab] = send_b[e]
        start, wait = spread(
            lambda peer: send_b.at[e], recv_b.at[e], b_ss, b_rs, 1 + e, "slab", slab, nslab
        )
        start()
        return wait

    def finish(e):
        part = recv_b[e, 0].astype(F32)
        for k in range(1, nslab):
            part = part + recv_b[e, k].astype(F32)
        gw_ref[1 - e] = part[0:blk] * pixel_scale

    send_c[...] = jnp.zeros_like(send_c)
    weight_grad(midt, b2)
    second = scatter(0)

    def stage_grad_one(i):
        y = conv(b2, 2, i)
        for k in range(2):
            r = 2 * i + k
            put(b1, r + 1, (y[k] * slope1[r]).astype(BF16))

    middle = 1 + (npair - 2) // 2
    loop(1, middle, stage_grad_one, 3)
    second.wait()
    second_wait = chips(0)
    to_core(small_c, small_rc, 0).wait()
    small_a[...] = (small_c[...].astype(F32) + small_rc[...].astype(F32)).astype(BF16)
    small_ra[chip] = small_a[...]
    small_start, small_wait = to_chips(lambda peer: small_a, small_ra, 0)
    small_start()
    loop(middle, npair - 1, stage_grad_one, 3)
    halo_wait(b2, 3)
    ends(stage_grad_one)
    halo_start(b1, 4)

    weight_grad(actt, b1)
    first = scatter(1)

    def stage_latents(i):
        y = conv(b1, 3, i)
        done = []
        for k in range(2):
            r = 2 * i + k
            g = y[k] * slope0[r]
            own = b2[r + 1, 1:t_count + 1].reshape(width, C).astype(F32)
            done.append((own + g).astype(BF16))
        z = dot(permt[...], jnp.concatenate(done, axis=1)).astype(BF16)
        for k in range(2):
            glp[2 * i + k] = z[:, k * C:(k + 1) * C]

    def latents_group(lo, hi):
        loop(lo, hi, stage_latents, hi - lo)
        for i in range(lo, hi):
            latents_out(i).start()

    latents_group(1, 2)
    first.wait()
    first_wait = chips(1)
    small_wait()
    part = small_ra[0].astype(F32)
    for k in range(1, nchip):
        part = part + small_ra[k].astype(F32)
    small_b[...] = part.astype(BF16)
    small_rb[slab] = small_b[...]
    small_b_start, small_b_wait = spread(
        lambda peer: small_b, small_rb, b_ss, b_rs, 0, "slab", slab, nslab
    )
    small_b_start()
    second_wait()
    second_b_wait = gather(0)
    latents_group(2, npair - 1)
    first_wait()
    first_b_wait = gather(1)
    halo_wait(b1, 4)
    ends(stage_latents)
    ends(lambda i: latents_out(i).start())

    small_b_wait()
    part = small_rb[0].astype(F32)
    for k in range(1, nslab):
        part = part + small_rb[k].astype(F32)
    part = part * pixel_scale
    gn_ref[0] = part[9:10]
    gn_ref[1] = part[10:11]
    for p in range(3):
        for q in range(3):
            at = (2 - p) * 16 + q * 3
            gci_ref[:, (3 * p + q) * C:(3 * p + q + 1) * C] = part[at:at + 3]
    second_b_wait()
    finish(0)
    first_b_wait()
    finish(1)
    loop(0, npair, lambda i: latents_out(i).wait())


def unload(parts, gl_in, gw_in, gci_in, gn_in, gw1, gw2, gci, gg, gb, gl, gl_buf, gw_buf, gci_buf, gn_buf, sem):
    step = gl_buf.shape[0] // parts
    moves = [(gw_in.at[0], gw_buf.at[0], gw1), (gw_in.at[1], gw_buf.at[1], gw2), (gci_in, gci_buf, gci)]
    moves += [(gn_in.at[0], gn_buf.at[0], gg), (gn_in.at[1], gn_buf.at[1], gb)]
    for i in range(parts):
        rows = pl.ds(i * step, step)
        moves.append((gl_in.at[rows], gl_buf.at[rows], gl.at[rows]))
    into = [pltpu.make_async_copy(m[0], m[1], sem.at[0, i]) for i, m in enumerate(moves)]
    back = [pltpu.make_async_copy(m[1], m[2], sem.at[1, i]) for i, m in enumerate(moves)]
    order = list(range(5, 5 + parts)) + list(range(5))
    for i in order:
        into[i].start()
    for i in order:
        into[i].wait()
        back[i].start()
    for i in order:
        back[i].wait()


def shards(
    latents, image_grad, heights, widths, buckets, bucket_scale,
    conv_first, conv_second, conv_image, norm_gain, norm_bias,
):
    images, rows, width, channels = latents.shape
    ndp = lax.axis_size("dp")
    nslab = lax.axis_size("slab")
    t_count = width // S
    pixel_scale = 1.0 / math.sqrt(images * ndp * rows * nslab * width)
    blk = 9 * C // ndp
    pad = -(-blk // 16) * 16
    vmem = pl.BlockSpec(memory_space=pltpu.VMEM)
    smem = pl.BlockSpec(memory_space=pltpu.SMEM)
    nchip = ndp // 2
    edge = (rows + 2, t_count + 2, S, C)
    wide = (rows + 4, t_count + 2, S, C)
    scratch = [
        pltpu.VMEM(image_grad.shape[1:], BF16),
        pltpu.VMEM(conv_first.shape, BF16),
        pltpu.VMEM(conv_second.shape, BF16),
        pltpu.SemaphoreType.DMA((3,)),
        pltpu.VMEM((rows, width, C), BF16),
        pltpu.VMEM((2, 2, width, C), BF16),
        pltpu.VMEM((rows, width, C), BF16),
        pltpu.VMEM((rows, width, C), F32),
        pltpu.VMEM((rows, width, C), F32),
        pltpu.VMEM((width, width), BF16),
        pltpu.VMEM((width, width), BF16),
        pltpu.VMEM((width, C), jnp.int32),
        pltpu.VMEM((rows, width, C), BF16),
        pltpu.VMEM(wide, BF16),
        pltpu.VMEM(edge, BF16),
        pltpu.VMEM((rows + 2, C, width), BF16),
        pltpu.VMEM((rows + 2, C, width), BF16),
        pltpu.VMEM((rows + 2, width, C), BF16),
        pltpu.VMEM((rows, width, C), F32),
        pltpu.VMEM((rows, width, C), F32),
        pltpu.VMEM((rows, width, C), BF16),
        pltpu.VMEM(edge, BF16),
        pltpu.VMEM(edge, BF16),
        pltpu.VMEM((4, 6 * C, 2 * C), BF16),
        pltpu.VMEM((4, 2, 2 * C, 2 * C), BF16),
        pltpu.VMEM((64, 2 * C), F32),
        pltpu.VMEM((64, 2 * C), BF16),
        pltpu.VMEM((width // C, 16 * rows, C), F32),
        pltpu.VMEM((rows + 2, 16, width), BF16),
        pltpu.VMEM((3 * C, 3 * C), F32),
        pltpu.VMEM((9 * C, C), F32),
        pltpu.VMEM((64, 2 * C), F32),
        pltpu.VMEM((4, 8, C), F32),
        pltpu.VMEM((2, 8, C), F32),
        pltpu.VMEM((2, nslab, 8, C), F32),
        pltpu.VMEM((2, 2, nchip, pad, C), BF16),
        pltpu.VMEM((2, nchip, pad, C), BF16),
        pltpu.VMEM((2, nchip, pad, C), BF16),
        pltpu.VMEM((2, nchip, pad, C), BF16),
        pltpu.VMEM((2, pad, C), BF16),
        pltpu.VMEM((2, nslab, pad, C), BF16),
        pltpu.VMEM((48, C), BF16),
        pltpu.VMEM((48, C), BF16),
        pltpu.VMEM((48, C), BF16),
        pltpu.VMEM((nchip, 48, C), BF16),
        pltpu.VMEM((48, C), BF16),
        pltpu.VMEM((nslab, 48, C), BF16),
        pltpu.SemaphoreType.DMA((2, rows // 2)),
        pltpu.SemaphoreType.DMA((5, 2)),
        pltpu.SemaphoreType.DMA((5, 2)),
        pltpu.SemaphoreType.DMA((2, nslab)),
        pltpu.SemaphoreType.DMA((2, nslab)),
        pltpu.SemaphoreType.DMA((3,)),
        pltpu.SemaphoreType.DMA((3,)),
        pltpu.SemaphoreType.DMA((3, nchip)),
        pltpu.SemaphoreType.DMA((3, nchip)),
        pltpu.SemaphoreType.DMA((3, nslab)),
        pltpu.SemaphoreType.DMA((3, nslab)),
    ]
    anywhere = pl.BlockSpec(memory_space=pl.ANY)
    staged = pl.pallas_call(
        functools.partial(kernel, ndp, nslab, rows, width, pixel_scale),
        out_shape=(
            jax.ShapeDtypeStruct((rows, width, C), BF16),
            jax.ShapeDtypeStruct((2, blk, C), F32),
            jax.ShapeDtypeStruct((3, 9 * C), F32),
            jax.ShapeDtypeStruct((2, 1, C), F32),
        ),
        in_specs=[anywhere, anywhere, smem, smem, smem, smem, anywhere, anywhere, vmem, vmem, vmem],
        out_specs=(anywhere, vmem, vmem, vmem),
        scratch_shapes=scratch,
        compiler_params=pltpu.CompilerParams(
            collective_id=0, has_side_effects=True, vmem_limit_bytes=60 * 2**20
        ),
        cost_estimate=pl.CostEstimate(
            flops=int(1.6e10), bytes_accessed=5 * 2**20, transcendentals=5 * 2**20
        ),
    )(
        latents[0], image_grad[0], heights, widths, buckets, bucket_scale,
        conv_first, conv_second, conv_image, norm_gain[None], norm_bias[None],
    )
    parts = 4
    gw1, gw2, gci, gg, gb, gl = pl.pallas_call(
        functools.partial(unload, parts),
        out_shape=(
            jax.ShapeDtypeStruct((blk, C), F32),
            jax.ShapeDtypeStruct((blk, C), F32),
            jax.ShapeDtypeStruct((3, 9 * C), F32),
            jax.ShapeDtypeStruct((1, C), F32),
            jax.ShapeDtypeStruct((1, C), F32),
            jax.ShapeDtypeStruct((rows, width, C), BF16),
        ),
        in_specs=[anywhere] * 4,
        out_specs=(anywhere,) * 6,
        scratch_shapes=[
            pltpu.VMEM((rows, width, C), BF16),
            pltpu.VMEM((2, blk, C), F32),
            pltpu.VMEM((3, 9 * C), F32),
            pltpu.VMEM((2, 1, C), F32),
            pltpu.SemaphoreType.DMA((2, parts + 5)),
        ],
        compiler_params=pltpu.CompilerParams(vmem_limit_bytes=60 * 2**20),
    )(*staged)
    return gw1, gw2, gci, gg[0], gb[0], gl[None]


def solution(mesh):
    placed = (
        P("dp", "slab", None, None),
        P("dp", None, "slab", None),
        P("dp"),
        P("dp"),
        P("dp"),
        P(),
        P(),
        P(),
        P(),
        P(),
        P(),
    )
    return jax.shard_map(
        shards,
        mesh=mesh,
        in_specs=placed,
        out_specs=(P("dp", None), P("dp", None), P(), P(), P(), P("dp", "slab", None, None)),
        check_vma=False,
    )
```
